256 devices in a mesh: dp: 32 (over y, z), seq: 8 (over x, core).
Axes of the slice: x: 4, y: 4, z: 8, core: 2. Of those that a mesh axis runs over, the one named last changes fastest.
Arguments:
- qkvu: bfloat16 [32, 1024, 4096], P('dp', 'seq'), may hold values from -40 to 40
- lengths: int32 [32], P('dp'), may hold values from 128 to 1024, as said below
- items: bfloat16 [32, 8, 64, 2048], P('dp', 'seq'), may hold values from -6 to 6
- send_list: int32 [32, 8, 32, 2], P('dp', 'seq'), may hold values from 0 to 63
- send_count: int32 [32, 8, 32], P('dp', 'seq'), may hold values from 0 to 2, as said below
- w_out: bfloat16 [1024, 1024], replicated, may hold values from -0.1875 to 0.1875
- gain: float32 [1024], replicated, may hold values from 0.1 to 1.9
- g_hist: bfloat16 [32, 1024, 1024], P('dp', 'seq'), may hold values from -6 to 6
- g_tgt: bfloat16 [32, 8, 32, 2, 1024], P('dp', 'seq'), may hold values from -6 to 6
Outputs:
- hist_out: bfloat16 [32, 1024, 1024], P('dp', 'seq')
- tgt_out: bfloat16 [32, 8, 32, 2, 1024], P('dp', 'seq')
- d_qkvu: bfloat16 [32, 1024, 4096], P('dp', 'seq')
- d_items: bfloat16 [32, 8, 64, 2048], P('dp', 'seq')
- d_w2: float32 [1024, 1024], P(('dp', 'seq'))
The draws below stay inside these ranges and needn't reach their ends.
Inputs may be any that keep to these rules, and one draw needn't show every extreme that they name: `lengths`: some user fills all 1024 rows in every draw. `send_count`: in every draw some receiving dp index gets 2 rows from every sender.
All inputs are finite; a program needn't handle non-finite values.
Results may differ from the reference program's by a relative error of at most 0.015.
Values may be sent and summed in bfloat16 or wider, within the bound.
A program may use at most 128 MiB of HBM per device.

```python
import math
import jax
import jax.numpy as jnp
from jax import lax

D = 1024
HEADS = 16
HD = 64
CAP = 2
ITEM_DEV = 64
SEQLEN = 1024
USERS = 32
SEATS = 8


def draw_qkvu(key, part):
    key = jax.random.fold_in(key, 11)
    first, second = jax.random.split(key, 2)
    spread = jax.random.uniform(second, (D,), jnp.float32, 0.0, 1.0)
    column = jnp.concatenate([jnp.ones((D,), jnp.float32), jnp.exp(spread * math.log(10.0)), jnp.ones((2 * D,), jnp.float32)])
    base = jnp.clip(jax.random.normal(first, (USERS, SEQLEN, 4 * D), jnp.float32), -4.0, 4.0)
    return (base * column[None, None, :]).astype(jnp.bfloat16)


def draw_lengths(key, part):
    key = jax.random.fold_in(key, 23)
    first, second = jax.random.split(key)
    drawn = jax.random.randint(first, (USERS,), SEQLEN // 8, SEQLEN + 1)
    longest = jax.random.randint(second, (), 0, USERS)
    return jnp.where(jnp.arange(USERS) == longest, SEQLEN, drawn).astype(jnp.int32)


def draw_send_count(key, part):
    key = jax.random.fold_in(key, 37)
    first, second = jax.random.split(key)
    drawn = jax.random.randint(first, (USERS, SEATS, USERS), 0, CAP + 1)
    busiest = jax.random.randint(second, (), 0, USERS)
    return jnp.where(jnp.arange(USERS)[None, None, :] == busiest, CAP, drawn).astype(jnp.int32)


def with_ends(array, own_key, smallest, top_value):
    place = [jax.random.randint(jax.random.fold_in(own_key, axis), (), 0, length) for axis, length in enumerate(array.shape)]
    widest = array.shape.index(max(array.shape))
    beside = place[:widest] + [(place[widest] + 1) % array.shape[widest]] + place[widest + 1:]
    return array.at[tuple(place)].set(smallest).at[tuple(beside)].set(top_value)


def steps_of(key, dims, pieces, smallest, largest):
    loudness, own = 1.0, jax.random.fold_in(key, 6)
    for position, blocks in pieces:
        heights = jnp.exp(jax.random.uniform(jax.random.fold_in(own, position), (blocks,), jnp.float32, smallest / len(pieces), largest / len(pieces)))
        loudness = loudness * jnp.repeat(heights, dims[position] // blocks).reshape([-1 if axis == position else 1 for axis in range(len(dims))])
    return loudness


def bell_draw(stream_key, shape, deviation, most, pieces=(), held_as=jnp.bfloat16):
    level = steps_of(stream_key, shape, pieces, -0.22, 0.18) if pieces else 1.0
    result = jax.random.normal(stream_key, shape, jnp.float32) * deviation * level
    return jnp.minimum(jnp.maximum(result, -most), most).astype(held_as)


def setup_inputs(seed: int = 0) -> dict:
    streams_of = jax.random.split(jax.random.key(seed), 10)
    return {
        "qkvu": draw_qkvu(jax.random.fold_in(streams_of[9], 71), 0),
        "lengths": draw_lengths(jax.random.fold_in(streams_of[9], 71), 0),
        "items": bell_draw(streams_of[2], (USERS, SEATS, ITEM_DEV, 2 * D), 1.0, 6.0, ((0, 32), (1, 8))),
        "send_list": with_ends(jax.random.randint(streams_of[3], (USERS, SEATS, USERS, CAP), 0, ITEM_DEV), jax.random.fold_in(streams_of[3], 1), 0, ITEM_DEV - 1).astype(jnp.int32),
        "send_count": draw_send_count(jax.random.fold_in(streams_of[9], 71), 0),
        "w_out": bell_draw(streams_of[5], (D, D), D ** -0.5, 0.1875),
        "gain": jnp.clip(1.0 + 0.18 * jax.random.normal(streams_of[6], (D,), jnp.float32), 0.1, 1.9),
        "g_hist": bell_draw(streams_of[7], (USERS, SEQLEN, D), 1.0, 6.0, ((0, 32), (1, 8))),
        "g_tgt": bell_draw(streams_of[8], (USERS, SEATS, USERS, CAP, D), 1.0, 6.0, ((0, 32), (1, 8))),
    }


def forward_tiles(queries, query_pos, query_live, keys, values, length):
    count, heads, depth = queries.shape
    span = keys.shape[0]
    query_step = math.gcd(count, 512)
    key_advance = math.gcd(span, 512)
    scale = depth ** (-0.5)

    def one_block(inputs):
        query_tile, pos_tile, live_tile = inputs
        query_float = query_tile.astype(jnp.float32)

        def add_tile(index, total):
            offset_begin = (index * key_advance).astype(jnp.int32)
            key_tile = lax.dynamic_slice_in_dim(keys, offset_begin, key_advance, 0).astype(jnp.float32)
            value_tile = lax.dynamic_slice_in_dim(values, offset_begin, key_advance, 0).astype(jnp.float32)
            key_pos = offset_begin + jnp.arange(key_advance, dtype=jnp.int32)
            allowed = (key_pos[None, :] <= pos_tile[:, None]) & (key_pos[None, :] < length) & live_tile[:, None]
            score = scale * jnp.einsum('qhe,khe->hqk', query_float, key_tile)
            weight = jnp.where(allowed[None], score * jax.nn.sigmoid(score), 0.0).astype(jnp.bfloat16)
            return total + jnp.einsum('hqk,khe->qhe', weight.astype(jnp.float32), value_tile)
        return lax.fori_loop(0, span // key_advance, add_tile, jnp.zeros((query_step, heads, depth), jnp.float32))
    parts = (queries.reshape(count // query_step, query_step, heads, depth), query_pos.reshape(count // query_step, query_step), query_live.reshape(count // query_step, query_step))
    return lax.map(one_block, parts).reshape(count, heads, depth)

def backward_tiles(queries, grads, query_pos, query_live, keys, values, length):
    count, heads, depth = queries.shape
    span = keys.shape[0]
    query_step = math.gcd(count, 512)
    key_advance = math.gcd(span, 512)
    scale = depth ** (-0.5)

    def query_round(index, carry):
        grad_query, grad_key, grad_value = carry
        first = (index * query_step).astype(jnp.int32)
        query_float = lax.dynamic_slice_in_dim(queries, first, query_step, 0).astype(jnp.float32)
        grad_float = lax.dynamic_slice_in_dim(grads, first, query_step, 0).astype(jnp.float32)
        pos_tile = lax.dynamic_slice_in_dim(query_pos, first, query_step, 0)
        live_tile = lax.dynamic_slice_in_dim(query_live, first, query_step, 0)

        def key_cycle(key_index, inner_loop):
            query_part, key_sums, value_sums = inner_loop
            offset_begin = (key_index * key_advance).astype(jnp.int32)
            key_tile = lax.dynamic_slice_in_dim(keys, offset_begin, key_advance, 0).astype(jnp.float32)
            value_tile = lax.dynamic_slice_in_dim(values, offset_begin, key_advance, 0).astype(jnp.float32)
            key_pos = offset_begin + jnp.arange(key_advance, dtype=jnp.int32)
            allowed = (key_pos[None, :] <= pos_tile[:, None]) & (key_pos[None, :] < length) & live_tile[:, None]
            score = scale * jnp.einsum('qhe,khe->hqk', query_float, key_tile)
            sigma = jax.nn.sigmoid(score)
            weight = jnp.where(allowed[None], score * sigma, 0.0).astype(jnp.bfloat16)
            d_weight = jnp.einsum('qhe,khe->hqk', grad_float, value_tile)
            d_score = jnp.where(allowed[None], d_weight * sigma * (1.0 + score * (1.0 - sigma)), 0.0).astype(jnp.bfloat16)
            d_score_float = d_score.astype(jnp.float32)
            query_part = query_part + scale * jnp.einsum('hqk,khe->qhe', d_score_float, key_tile)
            key_term = scale * jnp.einsum('hqk,qhe->khe', d_score_float, query_float)
            value_term = jnp.einsum('hqk,qhe->khe', weight.astype(jnp.float32), grad_float)
            key_sums = lax.dynamic_update_slice_in_dim(key_sums, lax.dynamic_slice_in_dim(key_sums, offset_begin, key_advance, 0) + key_term, offset_begin, 0)
            value_sums = lax.dynamic_update_slice_in_dim(value_sums, lax.dynamic_slice_in_dim(value_sums, offset_begin, key_advance, 0) + value_term, offset_begin, 0)
            return (query_part, key_sums, value_sums)
        start_carry = (jnp.zeros((query_step, heads, depth), jnp.float32), grad_key, grad_value)
        query_part, grad_key, grad_value = lax.fori_loop(0, span // key_advance, key_cycle, start_carry)
        grad_query = lax.dynamic_update_slice_in_dim(grad_query, query_part, first, 0)
        return (grad_query, grad_key, grad_value)
    zeros_query = jnp.zeros((count, heads, depth), jnp.float32)
    zeros_key = jnp.zeros((span, heads, depth), jnp.float32)
    return lax.fori_loop(0, count // query_step, query_round, (zeros_query, zeros_key, zeros_key))

def norm_rows(attended, gain, gate):
    values = attended.astype(jnp.float32)
    centred = values - lax.optimization_barrier(jnp.mean(values, axis=1, keepdims=True))
    inverse = lax.rsqrt(lax.optimization_barrier(jnp.mean(centred * centred, axis=1, keepdims=True)) + 1e-05)
    norm_result = centred * inverse
    gated = (norm_result * gain[None, :] * gate.astype(jnp.float32)).astype(jnp.bfloat16)
    return (gated, norm_result, inverse)

def norm_back(d_gated, norm_result, inverse, gain, gate):
    scaled = d_gated * gain[None, :]
    d_gate = (scaled * norm_result).astype(jnp.bfloat16)
    d_norm = scaled * gate.astype(jnp.float32)
    d_att = inverse * (d_norm - lax.optimization_barrier(jnp.mean(d_norm, axis=1, keepdims=True)) - norm_result * lax.optimization_barrier(jnp.mean(d_norm * norm_result, axis=1, keepdims=True)))
    return (d_gate, d_att.astype(jnp.bfloat16))

def reference(qkvu, lengths, items, send_list, send_count, w_out, gain, g_hist, g_tgt):
    sender = jnp.arange(USERS, dtype=jnp.int32)[:, None, None, None]
    seat = jnp.arange(SEATS, dtype=jnp.int32)[None, :, None, None]
    picked = items[sender, seat, send_list]
    live = jnp.arange(CAP, dtype=jnp.int32)[None, None, None, :] < send_count[..., None]
    picked = jnp.where(live[..., None], picked, jnp.zeros_like(picked)).astype(jnp.bfloat16)
    target_rows = jnp.transpose(picked, (2, 1, 0, 3, 4)).reshape(USERS, SEATS * USERS * CAP, 2 * D)
    cot_targets = g_tgt.reshape(USERS, SEATS * USERS * CAP, D)

    def one_user(total, inputs):
        history, length, targets, cot_hist, cot_tgt = inputs
        gate = history[:, :D]
        values = history[:, D:2 * D].reshape(SEQLEN, HEADS, HD)
        queries = history[:, 2 * D:3 * D].reshape(SEQLEN, HEADS, HD)
        keys = history[:, 3 * D:].reshape(SEQLEN, HEADS, HD)
        target_query = targets[:, :D].reshape(-1, HEADS, HD)
        target_gate = targets[:, D:]
        slots = targets.shape[0]
        hist_pos = jnp.arange(SEQLEN, dtype=jnp.int32)
        hist_live = hist_pos < length
        target_pos = jnp.full((slots,), SEQLEN, jnp.int32)
        target_live = jnp.ones((slots,), bool)
        att_hist = forward_tiles(queries, hist_pos, hist_live, keys, values, length).astype(jnp.bfloat16).reshape(SEQLEN, D)
        att_tgt = forward_tiles(target_query, target_pos, target_live, keys, values, length).astype(jnp.bfloat16).reshape(slots, D)
        history_gated, normed_hist, inverse_hist = norm_rows(att_hist, gain, gate)
        gated_tgt, normed_tgt, inverse_tgt = norm_rows(att_tgt, gain, target_gate)
        out_hist = jnp.dot(history_gated, w_out, preferred_element_type=jnp.float32).astype(jnp.bfloat16)
        out_tgt = jnp.dot(gated_tgt, w_out, preferred_element_type=jnp.float32).astype(jnp.bfloat16)
        dz_hist = jnp.dot(cot_hist, w_out.T, preferred_element_type=jnp.float32)
        dz_tgt = jnp.dot(cot_tgt, w_out.T, preferred_element_type=jnp.float32)
        du_hist, datt_hist = norm_back(dz_hist, normed_hist, inverse_hist, gain, gate)
        du_tgt, datt_tgt = norm_back(dz_tgt, normed_tgt, inverse_tgt, gain, target_gate)
        gq_hist, gk_hist, gv_hist = backward_tiles(queries, datt_hist.reshape(SEQLEN, HEADS, HD), hist_pos, hist_live, keys, values, length)
        gq_tgt, gk_tgt, gv_tgt = backward_tiles(target_query, datt_tgt.reshape(slots, HEADS, HD), target_pos, target_live, keys, values, length)
        d_rows = jnp.concatenate([du_hist, (gv_hist + gv_tgt).astype(jnp.bfloat16).reshape(SEQLEN, D), gq_hist.astype(jnp.bfloat16).reshape(SEQLEN, D), (gk_hist + gk_tgt).astype(jnp.bfloat16).reshape(SEQLEN, D)], axis=1)
        d_targets = jnp.concatenate([gq_tgt.astype(jnp.bfloat16).reshape(slots, D), du_tgt], axis=1)
        total = total + jnp.dot(history_gated.T, cot_hist, preferred_element_type=jnp.float32)
        total = total + jnp.dot(gated_tgt.T, cot_tgt, preferred_element_type=jnp.float32)
        return (total, (out_hist, out_tgt, d_rows, d_targets))
    start_total = jnp.zeros((D, D), jnp.float32)
    total, results = lax.scan(one_user, start_total, (qkvu, lengths, target_rows, g_hist, cot_targets))
    hist_out, tgt_out, d_qkvu, d_targets = results
    tgt_out = tgt_out.reshape(USERS, SEATS, USERS, CAP, D)
    returned = jnp.transpose(d_targets.reshape(USERS, SEATS, USERS, CAP, 2 * D), (2, 1, 0, 3, 4))
    table = (send_list[..., None] == jnp.arange(ITEM_DEV, dtype=jnp.int32)) & live[..., None]
    d_items = jnp.einsum('hsgcr,hsgcf->hsrf', table.astype(jnp.float32), returned.astype(jnp.float32)).astype(jnp.bfloat16)
    d_w2 = total * (USERS * SEQLEN) ** (-0.5)
    return (hist_out, tgt_out, d_qkvu, d_items, d_w2)
```

```python
import jax
import jax.numpy as jnp
from jax import lax
from jax.experimental import pallas as pl
from jax.experimental.pallas import tpu as pltpu
from jax.sharding import PartitionSpec as P

BF = jnp.bfloat16
F32 = jnp.float32
MESH = pl.DeviceIdType.MESH

D = 1024
SEQ = 8
DP = 32
NY = 4
NZ = 8
ROWS = 128
SLOTS = 64
HIST = 1024
ALL = 1536
TILE = 256
WIDE = 2 * TILE

(PK, PQ, PV, PT, PTQ, PAH, PAT, PDH, PDT, PGT, PQS, PQD, PGQ, PGK, PGV, PC, PY, PZ, PX, NPH) = range(20)
(LIN, LW, LCOT, LU, LHO, LTO, LDU, LGR, LDI, LDW, NLOC) = range(11)


def dot(a, b):
    return lax.dot_general(a, b, (((1,), (0,)), ((), ())), preferred_element_type=F32)


def dot_nt(a, b):
    return lax.dot_general(a, b, (((1,), (1,)), ((), ())), preferred_element_type=F32)


def dot_tn(a, b):
    return lax.dot_general(a, b, (((0,), (0,)), ((), ())), preferred_element_type=F32)


def one_hot(condition):
    return jnp.where(condition, 1.0, 0.0).astype(BF)


def kernel(
    code, length_ref, qkvu, items, w_hbm, gain, gh_hbm, gt_hbm,
    ho_out, to_out, dqkvu_out, di_out, dw_out,
    kraw, vraw, qraw, qs, kst, vst, wst, gst, dsc,
    u_v, w_v, cot, dz, sel_t, tsend, trecv, tq, tgate,
    o_h, att_r, datt, da_raw, da, gated, outs, du_h, dgt, zg, rg, dqt, yq, zq, rq,
    gq, gk, gv, di, p_send, p_own, c_recv, y_send, y_own, y_recv, z_send, z_own, z_recv, x_send, x_recv, dw,
    ssem, rsem, lsem,
):
    g = lax.axis_index("dp")
    s = lax.axis_index("seq")
    y, z = lax.div(g, NZ), lax.rem(g, NZ)
    core = lax.rem(s, 2)
    length = length_ref[0]

    def rows_at(index, size):
        return pl.ds(pl.multiple_of(index * size, size), size)

    barrier = pltpu.get_barrier_semaphore()

    def greet_dp(d, carry):
        pl.semaphore_signal(barrier, inc=1, device_id={"dp": lax.rem(g + d, DP)}, device_id_type=MESH)
        return carry

    for d in range(1, SEQ):
        pl.semaphore_signal(barrier, inc=1, device_id={"seq": lax.rem(s + d, SEQ)}, device_id_type=MESH)
    lax.fori_loop(1, DP, greet_dp, 0)

    def local(src, dst, sem):
        copy = pltpu.make_async_copy(src, dst, lsem.at[sem])
        copy.start()

    def local_wait(ref, sem):
        pltpu.make_async_copy(ref, ref, lsem.at[sem]).wait()

    def send(src, dst, phase, device):
        pltpu.make_async_remote_copy(
            src_ref=src, dst_ref=dst, send_sem=ssem.at[phase], recv_sem=rsem.at[phase],
            device_id=device, device_id_type=MESH,
        ).start()

    def seq_send(phase, src, dst):
        for d in range(1, SEQ):
            p = lax.rem(s + d, SEQ)
            send(src(p), dst, phase, {"seq": p})

    def got(ref, phase):
        pltpu.make_async_copy(ref, ref, rsem.at[phase]).wait()

    def sent(ref, phase):
        pltpu.make_async_copy(ref, ref, ssem.at[phase]).wait()

    for base, buf in ((3 * D, kraw), (2 * D, qraw), (D, vraw)):
        local(qkvu.at[:, pl.ds(pl.multiple_of(base + s * 128, 128), 128)], buf.at[rows_at(s, ROWS)], LIN)
    local(w_hbm, w_v, LW)
    local(gh_hbm, cot.at[pl.ds(0, ROWS)], LCOT)
    local(gt_hbm, cot.at[pl.ds(ROWS, SLOTS)], LCOT)
    local(qkvu.at[:, pl.ds(0, D)], u_v, LU)

    sel_t[...] = one_hot(lax.broadcasted_iota(jnp.int32, (512, 512), 0) == code[...])
    stacked = jnp.concatenate(
        [
            jnp.concatenate([items[:, 128 * k : 128 * k + 128], items[:, D + 128 * k : D + 128 * k + 128]], axis=1)
            for k in range(SEQ)
        ],
        axis=0,
    )
    tsend[...] = dot_tn(sel_t[...], stacked).astype(BF)

    pl.semaphore_wait(barrier, SEQ - 1 + DP - 1)

    def dp_send(phase, src, dst):
        def one(d, carry):
            p = lax.rem(g + d, DP)
            send(src.at[rows_at(p, 16)], dst.at[rows_at(g, 16)], phase, {"dp": p})
            return carry

        lax.fori_loop(1, DP, one, 0)

    for phase, base, buf in ((PK, 3 * D, kraw), (PQ, 2 * D, qraw), (PV, D, vraw)):
        seq_send(
            phase,
            lambda p, base=base: qkvu.at[:, pl.ds(pl.multiple_of(base + p * 128, 128), 128)],
            buf.at[rows_at(s, ROWS)],
        )
    dp_send(PT, tsend, trecv)
    trecv[rows_at(g, 16), :] = tsend[rows_at(g, 16), :]

    local_wait(w_v, LW)
    local_wait(cot, LCOT)
    local_wait(u_v, LU)
    dz[...] = dot_nt(cot[...], w_v[...])

    row512 = lax.broadcasted_iota(jnp.int32, (512, 512), 0)
    col512 = lax.broadcasted_iota(jnp.int32, (512, 512), 1)
    perm = one_hot(col512 == ((row512 & 63) >> 1) * 16 + (row512 >> 6) * 2 + (row512 & 1))
    perm_back = one_hot(row512 == ((col512 & 63) >> 1) * 16 + (col512 >> 6) * 2 + (col512 & 1))

    got(trecv.at[pl.ds(0, 496)], PT)
    arranged = dot(perm, trecv[...]).astype(BF)
    tq[...] = arranged[:, :128]
    for k in range(SEQ):
        tgate[:, 128 * k : 128 * k + 128] = arranged[64 * k : 64 * k + 64, 128:]
    target_rows = pl.ds(pl.multiple_of(HIST + s * SLOTS, SLOTS), SLOTS)
    seq_send(PTQ, lambda p: tq.at[rows_at(p, SLOTS)], qraw.at[target_rows])
    qraw[target_rows, :] = tq[rows_at(s, SLOTS), :]

    for buf in (kraw, qraw, vraw):
        local_wait(buf.at[pl.ds(0, ROWS)], LIN)
    lane = lax.broadcasted_iota(jnp.int32, (TILE, 128), 1)
    tile_row = lax.broadcasted_iota(jnp.int32, (TILE, 128), 0)

    def stack_heads(raw, out):
        for j in range(4):
            block = raw[TILE * j : TILE * j + TILE, :].astype(F32)
            live = tile_row < length - TILE * j
            out[WIDE * j : WIDE * j + TILE, :] = jnp.where(live & (lane < 64), block, 0.0).astype(BF)
            out[WIDE * j + TILE : WIDE * j + WIDE, :] = jnp.where(live & (lane >= 64), block, 0.0).astype(BF)

    got(kraw.at[pl.ds(0, 896)], PK)
    stack_heads(kraw, kst)
    got(qraw.at[pl.ds(0, 896)], PQ)
    for i in range(4):
        block = qraw[TILE * i : TILE * i + TILE, :].astype(F32) * 0.0625
        qs[TILE * i : TILE * i + TILE, :] = jnp.where(tile_row < length - TILE * i, block, 0.0).astype(BF)
    got(vraw.at[pl.ds(0, 896)], PV)
    stack_heads(vraw, vst)

    causal = (lax.broadcasted_iota(jnp.int32, (TILE, WIDE), 1) & (TILE - 1)) <= lax.broadcasted_iota(
        jnp.int32, (TILE, WIDE), 0
    )

    def forward(i):
        rows = slice(TILE * i, TILE * i + TILE)
        count = min(i, 3) + 1
        for j in range(count):
            cols = slice(WIDE * j, WIDE * j + WIDE)
            half = dot_nt(qs[rows, :], kst[cols, :])
            twice = 1.0 + jnp.tanh(half)
            weight = half * twice
            slope = 0.5 * twice * (1.0 - weight) + weight
            if i == j:
                weight = jnp.where(causal, weight, 0.0)
                slope = jnp.where(causal, slope, 0.0)
            wst[rows, cols] = weight.astype(BF)
            gst[rows, cols] = slope.astype(BF)
        o_h[rows, :] = dot(wst[rows, : WIDE * count], vst[: WIDE * count, :]).astype(BF)

    for i in range(4):
        forward(i)
    seq_send(PAH, lambda p: o_h.at[rows_at(p, ROWS)], att_r.at[s, pl.ds(0, ROWS)])
    att_r[s, pl.ds(0, ROWS), :] = o_h[rows_at(s, ROWS), :]

    got(qraw.at[pl.ds(HIST, 448)], PTQ)
    for i in range(4, 6):
        rows = slice(TILE * i, TILE * i + TILE)
        qs[rows, :] = (qraw[rows, :].astype(F32) * 0.0625).astype(BF)
        forward(i)
    seq_send(
        PAT,
        lambda p: o_h.at[pl.ds(pl.multiple_of(HIST + p * SLOTS, SLOTS), SLOTS)],
        att_r.at[s, pl.ds(ROWS, SLOTS)],
    )
    att_r[s, pl.ds(ROWS, SLOTS), :] = o_h[target_rows, :]

    def norm(first, gate_ref, gate_first, du_ref):
        rows = pl.ds(pl.multiple_of(first, 32), 32)
        gate_rows = pl.ds(pl.multiple_of(gate_first, 32), 32)
        att = jnp.concatenate([att_r[k, rows, :] for k in range(SEQ)], axis=1).astype(F32)
        centred = att - jnp.mean(att, axis=1, keepdims=True)
        inverse = lax.rsqrt(jnp.mean(centred * centred, axis=1, keepdims=True) + 1e-05)
        normed = centred * inverse
        gate = gate_ref[gate_rows, :].astype(F32)
        gated[rows, :] = (normed * gain[...] * gate).astype(BF)
        scaled = dz[rows, :] * gain[...]
        du_ref[gate_rows, :] = (scaled * normed).astype(BF)
        d_norm = scaled * gate
        d_att = inverse * (
            d_norm
            - jnp.mean(d_norm, axis=1, keepdims=True)
            - normed * jnp.mean(d_norm * normed, axis=1, keepdims=True)
        )
        d_att = d_att.astype(BF)
        for k in range(SEQ):
            datt[k, rows, :] = d_att[:, 128 * k : 128 * k + 128]

    def norm_hist(r, carry):
        norm(r * 32, u_v, r * 32, du_h)
        return carry

    def norm_tgt(r, carry):
        norm(ROWS + r * 32, tgate, r * 32, dgt)
        return carry

    got(att_r.at[pl.ds(0, 7), pl.ds(0, ROWS)], PAH)
    lax.fori_loop(0, 4, norm_hist, 0)
    seq_send(PDH, lambda p: datt.at[p, pl.ds(0, ROWS)], da_raw.at[rows_at(s, ROWS)])
    da_raw[rows_at(s, ROWS), :] = datt[s, pl.ds(0, ROWS), :]
    local(du_h, dqkvu_out.at[:, pl.ds(0, D)], LDU)

    got(att_r.at[pl.ds(0, 7), pl.ds(ROWS, SLOTS)], PAT)
    lax.fori_loop(0, 2, norm_tgt, 0)
    seq_send(PDT, lambda p: datt.at[p, pl.ds(ROWS, SLOTS)], da_raw.at[target_rows])
    da_raw[target_rows, :] = datt[s, pl.ds(ROWS, SLOTS), :]

    gate_stack = jnp.concatenate([dgt[:, 128 * k : 128 * k + 128] for k in range(SEQ)], axis=0)
    zg[...] = dot(perm_back, gate_stack).astype(BF)
    dp_send(PGT, zg, rg)
    rg[rows_at(g, 16), :] = zg[rows_at(g, 16), :]

    other = 1 - core
    p_send[...] = dot_tn(gated[...], cot[:, rows_at(other, 512)]).astype(BF)
    send(p_send, c_recv, PC, {"seq": s + 1 - 2 * core})
    p_own[...] = dot_tn(gated[...], cot[:, rows_at(core, 512)])
    outs[...] = dot(gated[...], w_v[...]).astype(BF)
    local(outs.at[pl.ds(0, ROWS)], ho_out, LHO)
    local(outs.at[pl.ds(ROWS, SLOTS)], to_out, LTO)

    def backward(i):
        rows = slice(TILE * i, TILE * i + TILE)
        count = min(i, 3) + 1
        for j in range(count):
            cols = slice(WIDE * j, WIDE * j + WIDE)
            d_weight = dot_nt(da[rows, :], vst[cols, :])
            dsc[rows, cols] = (d_weight * gst[rows, cols].astype(F32)).astype(BF)
        return (dot(dsc[rows, : WIDE * count], kst[: WIDE * count, :]) * 0.125).astype(BF)

    got(da_raw.at[pl.ds(HIST, 448)], PDT)
    da[HIST:ALL, :] = da_raw[HIST:ALL, :]
    for i in range(4, 6):
        dqt[TILE * (i - 4) : TILE * (i - 3), :] = backward(i)
    seq_send(PQS, lambda p: dqt.at[rows_at(p, SLOTS)], yq.at[rows_at(s, SLOTS)])
    yq[rows_at(s, SLOTS), :] = dqt[rows_at(s, SLOTS), :]

    got(c_recv, PC)
    for d in range(1, NY + 1):
        yp = lax.rem(y + d, NY)
        rows = rows_at(yp, 256)
        total = p_own[rows, :] + c_recv[rows, :].astype(F32)
        if d < NY:
            y_send[yp] = total.astype(BF)
            send(y_send.at[yp], y_recv.at[y], PY, {"dp": yp * NZ + z})
        else:
            y_own[...] = total

    got(da_raw.at[pl.ds(0, 896)], PDH)
    for i in range(4):
        rows = slice(TILE * i, TILE * i + TILE)
        da[rows, :] = jnp.where(tile_row < length - TILE * i, da_raw[rows, :].astype(F32), 0.0).astype(BF)
    for i in range(4):
        gq[TILE * i : TILE * i + TILE, :] = backward(i)

    def grads_send(phase, buf, base):
        place = dqkvu_out.at[:, pl.ds(pl.multiple_of(base + s * 128, 128), 128)]
        seq_send(phase, lambda p: buf.at[rows_at(p, ROWS)], place)
        local(buf.at[rows_at(s, ROWS)], place, LGR)

    grads_send(PGQ, gq, 2 * D)

    def key_sum(left, right, j):
        both = dot_tn(left[TILE * j : ALL, WIDE * j : WIDE * j + WIDE], right[TILE * j : ALL, :])
        return jnp.where(lane < 64, both[:TILE, :], both[TILE:, :])

    for j in range(4):
        gk[TILE * j : TILE * j + TILE, :] = (key_sum(dsc, qs, j) * 2.0).astype(BF)
    grads_send(PGK, gk, 3 * D)
    for j in range(4):
        gv[TILE * j : TILE * j + TILE, :] = key_sum(wst, da, j).astype(BF)
    grads_send(PGV, gv, D)

    got(yq.at[pl.ds(0, 448)], PQS)
    zq[...] = dot(perm_back, yq[...]).astype(BF)
    dp_send(PQD, zq, rq)
    rq[rows_at(g, 16), :] = zq[rows_at(g, 16), :]

    got(y_recv.at[pl.ds(0, NY - 1)], PY)
    total = y_own[...]
    for d in range(1, NY):
        total = total + y_recv[lax.rem(y + d, NY)].astype(F32)
    y_own[...] = total
    for d in range(1, NZ):
        zp = lax.rem(z + d, NZ)
        z_send[zp] = y_own[rows_at(zp, 32), :].astype(BF)
        send(z_send.at[zp], z_recv.at[z], PZ, {"dp": y * NZ + zp})
    z_own[...] = y_own[rows_at(z, 32), :]

    got(rg.at[pl.ds(0, 496)], PGT)
    got(rq.at[pl.ds(0, 496)], PQD)
    returned = jnp.concatenate([rq[...], rg[...]], axis=1)
    d_items = dot(sel_t[...], returned).astype(BF)
    for k in range(SEQ):
        di[:, 128 * k : 128 * k + 128] = d_items[64 * k : 64 * k + 64, :128]
        di[:, D + 128 * k : D + 128 * k + 128] = d_items[64 * k : 64 * k + 64, 128:]
    local(di, di_out, LDI)

    got(z_recv.at[pl.ds(0, NZ - 1)], PZ)
    total = z_own[...]
    for d in range(1, NZ):
        total = total + z_recv[lax.rem(z + d, NZ)].astype(F32)
    x_send[...] = total
    seq_send(PX, lambda p: x_send.at[rows_at(lax.div(p, 2), 8)], x_recv.at[s])
    x_recv[s] = x_send[rows_at(lax.div(s, 2), 8), :]
    got(x_recv.at[pl.ds(0, SEQ - 1)], PX)
    halves = [x_recv[c] + x_recv[2 + c] + x_recv[4 + c] + x_recv[6 + c] for c in range(2)]
    full = jnp.concatenate(halves, axis=1) * (32768.0 ** -0.5)
    dw[...] = jnp.where(core == 0, full[:4, :], full[4:, :])
    local(dw, dw_out, LDW)

    for phase, buf in ((PGQ, gq), (PGK, gk), (PGV, gv)):
        got(buf.at[pl.ds(0, 896)], phase)
        sent(buf.at[pl.ds(0, 896)], phase)
        local_wait(buf.at[pl.ds(0, ROWS)], LGR)
    for phase, buf in ((PK, kraw), (PQ, qraw), (PV, vraw), (PAH, o_h), (PDH, da_raw)):
        sent(buf.at[pl.ds(0, 896)], phase)
    for phase, buf in ((PTQ, tq), (PAT, o_h), (PDT, da_raw), (PQS, dqt)):
        sent(buf.at[pl.ds(0, 448)], phase)
    for phase, buf in ((PT, tsend), (PGT, zg), (PQD, zq)):
        sent(buf.at[pl.ds(0, 496)], phase)
    sent(p_send, PC)
    sent(y_send.at[pl.ds(0, NY - 1)], PY)
    sent(z_send.at[pl.ds(0, NZ - 1)], PZ)
    sent(x_recv.at[pl.ds(0, SEQ - 1)], PX)
    local_wait(du_h, LDU)
    local_wait(outs.at[pl.ds(0, ROWS)], LHO)
    local_wait(outs.at[pl.ds(ROWS, SLOTS)], LTO)
    local_wait(di, LDI)
    local_wait(dw, LDW)


def scratch():
    def vm(*shape, dtype=BF):
        return pltpu.VMEM(shape, dtype)

    return [
        vm(HIST, 128), vm(HIST, 128), vm(ALL, 128), vm(ALL, 128),
        vm(2 * HIST, 128), vm(2 * HIST, 128),
        vm(ALL, 2 * HIST), vm(ALL, 2 * HIST), vm(ALL, 2 * HIST),
        vm(ROWS, D), vm(D, D), vm(ROWS + SLOTS, D), vm(ROWS + SLOTS, D, dtype=F32),
        vm(512, 512), vm(512, 256), vm(512, 256), vm(512, 128), vm(SLOTS, D),
        vm(ALL, 128), vm(SEQ, ROWS + SLOTS, 128), vm(SEQ, ROWS + SLOTS, 128),
        vm(ALL, 128), vm(ALL, 128),
        vm(ROWS + SLOTS, D), vm(ROWS + SLOTS, D), vm(ROWS, D), vm(SLOTS, D),
        vm(512, 128), vm(512, 128), vm(512, 128), vm(512, 128), vm(512, 128), vm(512, 128),
        vm(HIST, 128), vm(HIST, 128), vm(HIST, 128), vm(SLOTS, 2 * D),
        vm(D, 512), vm(D, 512, dtype=F32), vm(D, 512),
        vm(NY, 256, 512), vm(256, 512, dtype=F32), vm(NY, 256, 512),
        vm(NZ, 32, 512), vm(32, 512, dtype=F32), vm(NZ, 32, 512),
        vm(32, 512, dtype=F32), vm(SEQ, 8, 512, dtype=F32), vm(4, D, dtype=F32),
        pltpu.SemaphoreType.DMA((NPH,)),
        pltpu.SemaphoreType.DMA((NPH,)),
        pltpu.SemaphoreType.DMA((NLOC,)),
    ]


def shards(qkvu, lengths, items, send_list, send_count, w_out, gain, g_hist, g_tgt):
    lists, counts = send_list[0, 0], send_count[0, 0]
    slot = lax.broadcasted_iota(jnp.int32, (DP, SEQ, 2), 2)
    block = lax.broadcasted_iota(jnp.int32, (DP, SEQ, 2), 1)
    code = jnp.where(slot < counts[:, None, None], block * SLOTS + lists[:, None, :], -1).reshape(1, 512)
    anywhere = pl.BlockSpec(memory_space=pl.ANY)
    vmem = pl.BlockSpec(memory_space=pltpu.VMEM)
    hist_out, tgt_out, d_qkvu, d_items, d_w2 = pl.pallas_call(
        kernel,
        out_shape=(
            jax.ShapeDtypeStruct((ROWS, D), BF),
            jax.ShapeDtypeStruct((SLOTS, D), BF),
            jax.ShapeDtypeStruct((ROWS, 4 * D), BF),
            jax.ShapeDtypeStruct((SLOTS, 2 * D), BF),
            jax.ShapeDtypeStruct((4, D), F32),
        ),
        in_specs=[vmem, pl.BlockSpec(memory_space=pltpu.SMEM), anywhere, vmem, anywhere, vmem, anywhere, anywhere],
        out_specs=(anywhere,) * 5,
        scratch_shapes=scratch(),
        compiler_params=pltpu.CompilerParams(
            collective_id=0, has_side_effects=True, vmem_limit_bytes=60 * 1024 * 1024
        ),
    )(code, lengths, qkvu[0], items[0, 0], w_out, gain.reshape(1, D), g_hist[0], g_tgt.reshape(SLOTS, D))
    return (
        hist_out[None],
        tgt_out.reshape(1, 1, DP, 2, D),
        d_qkvu[None],
        d_items[None, None],
        d_w2,
    )


def solution(mesh):
    in_specs = (
        P("dp", "seq", None),
        P("dp"),
        P("dp", "seq", None, None),
        P("dp", "seq", None, None),
        P("dp", "seq", None),
        P(),
        P(),
        P("dp", "seq", None),
        P("dp", "seq", None, None, None),
    )
    out_specs = (
        P("dp", "seq", None),
        P("dp", "seq", None, None, None),
        P("dp", "seq", None),
        P("dp", "seq", None, None),
        P(("dp", "seq"), None),
    )
    return jax.shard_map(shards, mesh=mesh, in_specs=in_specs, out_specs=out_specs, check_vma=False)
```

```python
import jax
import jax.numpy as jnp
from jax import lax
from jax.experimental import pallas as pl
from jax.experimental.pallas import tpu as pltpu
from jax.sharding import PartitionSpec as P

BF = jnp.bfloat16
F32 = jnp.float32
MESH = pl.DeviceIdType.MESH

D = 1024
SEQ = 8
DP = 32
NY = 4
NZ = 8
ROWS = 128
SLOTS = 64
HIST = 1024
ALL = 1536
TILE = 256
WIDE = 2 * TILE

(PK, PQ, PV, PT, PTQ, PAH, PAT, PDH, PDT, PGT, PQS, PQD, PGQ, PGK, PGV, PCO, PGA, PGB, PZ, PX, NPH) = range(21)
(LLI, LCO, LIT, LGA, LIN, LW, LCOT, LGT, LU, LHO, LTO, LDU, LGR, LDI, LDW, NLOC) = range(16)


def dot(a, b):
    return lax.dot_general(a, b, (((1,), (0,)), ((), ())), preferred_element_type=F32)


def dot_nt(a, b):
    return lax.dot_general(a, b, (((1,), (1,)), ((), ())), preferred_element_type=F32)


def dot_tn(a, b):
    return lax.dot_general(a, b, (((0,), (0,)), ((), ())), preferred_element_type=F32)


def one_hot(condition):
    return jnp.where(condition, 1.0, 0.0).astype(BF)


def kernel(
    lists_hbm, counts_hbm, length_ref, qkvu, items_hbm, w_hbm, gain_hbm, gh_hbm, gt_hbm,
    ho_out, to_out, dqkvu_out, di_out, dw_out,
    kraw, vraw, qraw, qs, kst, vst, wst, gst, dsc,
    lists, counts, items, gain, u_v, w_v, gt_v, to_v, rows32, cot, dz, sel_t, tsend, trecv, tq, tgate,
    o_h, att_r, datt, da_raw, da, gated, outs, du_h, dgt, zg, rg, dqt, yq, zq, rq,
    gq, gk, gv, di, cot_all, gated_all, y_own, z_send, z_own, z_recv, x_send, x_recv, dw,
    ssem, rsem, lsem,
):
    g = lax.axis_index("dp")
    s = lax.axis_index("seq")
    y, z = lax.div(g, NZ), lax.rem(g, NZ)
    core = lax.rem(s, 2)
    other = s + 1 - 2 * core
    mine = 2 * y + core
    length = length_ref[0]

    def rows_at(index, size):
        return pl.ds(pl.multiple_of(index * size, size), size)

    barrier = pltpu.get_barrier_semaphore()

    def greet_dp(d, carry):
        pl.semaphore_signal(barrier, inc=1, device_id={"dp": lax.rem(g + d, DP)}, device_id_type=MESH)
        return carry

    for d in range(1, SEQ):
        pl.semaphore_signal(barrier, inc=1, device_id={"seq": lax.rem(s + d, SEQ)}, device_id_type=MESH)
    lax.fori_loop(1, DP, greet_dp, 0)
    for d in range(1, NY):
        pl.semaphore_signal(
            barrier, inc=1, device_id={"dp": lax.rem(y + d, NY) * NZ + z, "seq": other}, device_id_type=MESH
        )

    def local(src, dst, sem):
        copy = pltpu.make_async_copy(src, dst, lsem.at[sem])
        copy.start()

    def local_wait(ref, sem):
        pltpu.make_async_copy(ref, ref, lsem.at[sem]).wait()

    def send(src, dst, phase, device):
        pltpu.make_async_remote_copy(
            src_ref=src, dst_ref=dst, send_sem=ssem.at[phase], recv_sem=rsem.at[phase],
            device_id=device, device_id_type=MESH,
        ).start()

    def seq_send(phase, src, dst):
        for d in range(1, SEQ):
            p = lax.rem(s + d, SEQ)
            send(src(p), dst, phase, {"seq": p})

    def got(ref, phase):
        pltpu.make_async_copy(ref, ref, rsem.at[phase]).wait()

    def sent(ref, phase):
        pltpu.make_async_copy(ref, ref, ssem.at[phase]).wait()

    local(lists_hbm, lists, LLI)
    local(counts_hbm, counts, LCO)
    local(items_hbm, items, LIT)
    local(gain_hbm, gain, LGA)
    for base, buf in ((3 * D, kraw), (2 * D, qraw), (D, vraw)):
        local(qkvu.at[:, pl.ds(pl.multiple_of(base + s * 128, 128), 128)], buf.at[rows_at(s, ROWS)], LIN)
    local(w_hbm, w_v, LW)
    local(gh_hbm, cot.at[pl.ds(0, ROWS)], LCOT)
    local(gt_hbm, gt_v, LGT)
    local(qkvu.at[:, pl.ds(0, D)], u_v, LU)

    local_wait(lists, LLI)
    local_wait(counts, LCO)
    lane512 = lax.broadcasted_iota(jnp.int32, (DP, 512), 1)
    spread = one_hot((lane512 >> 4) == lax.broadcasted_iota(jnp.int32, (DP, 512), 0))

    def spread_row(row):
        return dot(jnp.broadcast_to(row.astype(F32), (16, DP)).astype(BF), spread)[:1, :]

    slot = lax.broadcasted_iota(jnp.int32, (1, 512), 1)
    second = (slot & 1) == 1
    picked = jnp.where(second, spread_row(lists[1:2, :]), spread_row(lists[0:1, :]))
    live = spread_row(counts[...]) > jnp.where(second, 1.5, 0.5)
    code = jnp.where(live, picked + (((slot >> 1) & 7) * SLOTS).astype(F32), -1.0)
    sel_t[...] = one_hot(lax.broadcasted_iota(jnp.int32, (512, 512), 0).astype(F32) == code)
    local_wait(items, LIT)
    stacked = jnp.concatenate(
        [
            jnp.concatenate([items[:, 128 * k : 128 * k + 128], items[:, D + 128 * k : D + 128 * k + 128]], axis=1)
            for k in range(SEQ)
        ],
        axis=0,
    )
    tsend[...] = dot_tn(sel_t[...], stacked).astype(BF)

    pl.semaphore_wait(barrier, SEQ - 1 + DP - 1 + NY - 1)

    def dp_send(phase, src, dst):
        def one(d, carry):
            p = lax.rem(g + d, DP)
            send(src.at[rows_at(p, 16)], dst.at[rows_at(g, 16)], phase, {"dp": p})
            return carry

        lax.fori_loop(1, DP, one, 0)

    def columns_send(phase, base, buf):
        seq_send(
            phase, lambda p: qkvu.at[:, pl.ds(pl.multiple_of(base + p * 128, 128), 128)], buf.at[rows_at(s, ROWS)]
        )

    columns_send(PK, 3 * D, kraw)
    dp_send(PT, tsend, trecv)
    columns_send(PQ, 2 * D, qraw)
    columns_send(PV, D, vraw)
    trecv[rows_at(g, 16), :] = tsend[rows_at(g, 16), :]

    local_wait(w_v, LW)
    local_wait(cot.at[pl.ds(0, ROWS)], LCOT)
    local_wait(gt_v, LGT)
    for h in range(DP):
        rows32[2 * h : 2 * h + 2, :] = gt_v[h].astype(F32)
    cot[ROWS:, :] = rows32[...].astype(BF)
    dz[...] = dot_nt(cot[...], w_v[...])

    row512 = lax.broadcasted_iota(jnp.int32, (512, 512), 0)
    col512 = lax.broadcasted_iota(jnp.int32, (512, 512), 1)
    perm = one_hot(col512 == ((row512 & 63) >> 1) * 16 + (row512 >> 6) * 2 + (row512 & 1))
    perm_back = one_hot(row512 == ((col512 & 63) >> 1) * 16 + (col512 >> 6) * 2 + (col512 & 1))

    got(trecv.at[pl.ds(0, 496)], PT)
    arranged = dot(perm, trecv[...]).astype(BF)
    tq[...] = arranged[:, :128]
    for k in range(SEQ):
        tgate[:, 128 * k : 128 * k + 128] = arranged[64 * k : 64 * k + 64, 128:]
    target_rows = pl.ds(pl.multiple_of(HIST + s * SLOTS, SLOTS), SLOTS)
    seq_send(PTQ, lambda p: tq.at[rows_at(p, SLOTS)], qraw.at[target_rows])
    qraw[target_rows, :] = tq[rows_at(s, SLOTS), :]

    def group_send(phase, src, dst):
        for d in range(1, 2 * NY):
            r = lax.rem(mine + d, 2 * NY)
            ry, rc = lax.div(r, 2), lax.rem(r, 2)
            send(src(ry, rc), dst, phase, {"dp": ry * NZ + z, "seq": s - core + rc})

    group_send(PCO, lambda ry, rc: cot.at[:, rows_at(rc, 512)], cot_all.at[mine])
    cot_all[mine] = cot[:, rows_at(core, 512)]
    local_wait(u_v, LU)
    local_wait(gain, LGA)

    for buf in (kraw, qraw, vraw):
        local_wait(buf.at[pl.ds(0, ROWS)], LIN)
    lane = lax.broadcasted_iota(jnp.int32, (TILE, 128), 1)
    tile_row = lax.broadcasted_iota(jnp.int32, (TILE, 128), 0)

    def stack_heads(raw, out):
        for j in range(4):
            block = raw[TILE * j : TILE * j + TILE, :].astype(F32)
            live = tile_row < length - TILE * j
            out[WIDE * j : WIDE * j + TILE, :] = jnp.where(live & (lane < 64), block, 0.0).astype(BF)
            out[WIDE * j + TILE : WIDE * j + WIDE, :] = jnp.where(live & (lane >= 64), block, 0.0).astype(BF)

    got(kraw.at[pl.ds(0, 896)], PK)
    stack_heads(kraw, kst)
    got(qraw.at[pl.ds(0, 896)], PQ)
    for i in range(4):
        block = qraw[TILE * i : TILE * i + TILE, :].astype(F32) * 0.0625
        qs[TILE * i : TILE * i + TILE, :] = jnp.where(tile_row < length - TILE * i, block, 0.0).astype(BF)

    causal = (lax.broadcasted_iota(jnp.int32, (TILE, WIDE), 1) & (TILE - 1)) <= lax.broadcasted_iota(
        jnp.int32, (TILE, WIDE), 0
    )

    def scores(i):
        rows = slice(TILE * i, TILE * i + TILE)
        count = min(i, 3) + 1
        for j in range(count):
            cols = slice(WIDE * j, WIDE * j + WIDE)
            half = dot_nt(qs[rows, :], kst[cols, :])
            twice = 1.0 + jnp.tanh(half)
            weight = half * twice
            slope = 0.5 * twice * (1.0 - weight) + weight
            if i == j:
                weight = jnp.where(causal, weight, 0.0)
                slope = jnp.where(causal, slope, 0.0)
            wst[rows, cols] = weight.astype(BF)
            gst[rows, cols] = slope.astype(BF)

    def attend(i):
        rows = slice(TILE * i, TILE * i + TILE)
        count = min(i, 3) + 1
        o_h[rows, :] = dot(wst[rows, : WIDE * count], vst[: WIDE * count, :]).astype(BF)

    for i in range(4):
        scores(i)
    got(vraw.at[pl.ds(0, 896)], PV)
    stack_heads(vraw, vst)
    for i in range(4):
        attend(i)
    seq_send(PAH, lambda p: o_h.at[rows_at(p, ROWS)], att_r.at[s, pl.ds(0, ROWS)])
    att_r[s, pl.ds(0, ROWS), :] = o_h[rows_at(s, ROWS), :]

    got(qraw.at[pl.ds(HIST, 448)], PTQ)
    for i in range(4, 6):
        rows = slice(TILE * i, TILE * i + TILE)
        qs[rows, :] = (qraw[rows, :].astype(F32) * 0.0625).astype(BF)
        scores(i)
        attend(i)
    seq_send(
        PAT,
        lambda p: o_h.at[pl.ds(pl.multiple_of(HIST + p * SLOTS, SLOTS), SLOTS)],
        att_r.at[s, pl.ds(ROWS, SLOTS)],
    )
    att_r[s, pl.ds(ROWS, SLOTS), :] = o_h[target_rows, :]

    def norm(first, gate_ref, gate_first, du_ref):
        rows = pl.ds(pl.multiple_of(first, 32), 32)
        gate_rows = pl.ds(pl.multiple_of(gate_first, 32), 32)
        att = jnp.concatenate([att_r[k, rows, :] for k in range(SEQ)], axis=1).astype(F32)
        centred = att - jnp.mean(att, axis=1, keepdims=True)
        inverse = lax.rsqrt(jnp.mean(centred * centred, axis=1, keepdims=True) + 1e-05)
        normed = centred * inverse
        gate = gate_ref[gate_rows, :].astype(F32)
        gated[rows, :] = (normed * gain[...] * gate).astype(BF)
        scaled = dz[rows, :] * gain[...]
        du_ref[gate_rows, :] = (scaled * normed).astype(BF)
        d_norm = scaled * gate
        d_att = inverse * (
            d_norm
            - jnp.mean(d_norm, axis=1, keepdims=True)
            - normed * jnp.mean(d_norm * normed, axis=1, keepdims=True)
        )
        d_att = d_att.astype(BF)
        for k in range(SEQ):
            datt[k, rows, :] = d_att[:, 128 * k : 128 * k + 128]

    def norm_hist(r, carry):
        norm(r * 32, u_v, r * 32, du_h)
        return carry

    def norm_tgt(r, carry):
        norm(ROWS + r * 32, tgate, r * 32, dgt)
        return carry

    got(att_r.at[pl.ds(0, 7), pl.ds(0, ROWS)], PAH)
    lax.fori_loop(0, 4, norm_hist, 0)
    seq_send(PDH, lambda p: datt.at[p, pl.ds(0, ROWS)], da_raw.at[rows_at(s, ROWS)])
    da_raw[rows_at(s, ROWS), :] = datt[s, pl.ds(0, ROWS), :]
    local(du_h, dqkvu_out.at[:, pl.ds(0, D)], LDU)
    hist_rows = pl.ds(0, ROWS)
    slot_rows = pl.ds(ROWS, SLOTS)
    group_send(PGA, lambda ry, rc: gated.at[hist_rows, rows_at(ry, 256)], gated_all.at[mine, hist_rows])

    got(att_r.at[pl.ds(0, 7), pl.ds(ROWS, SLOTS)], PAT)
    lax.fori_loop(0, 2, norm_tgt, 0)
    seq_send(PDT, lambda p: datt.at[p, pl.ds(ROWS, SLOTS)], da_raw.at[target_rows])
    da_raw[target_rows, :] = datt[s, pl.ds(ROWS, SLOTS), :]

    gate_stack = jnp.concatenate([dgt[:, 128 * k : 128 * k + 128] for k in range(SEQ)], axis=0)
    zg[...] = dot(perm_back, gate_stack).astype(BF)
    dp_send(PGT, zg, rg)
    rg[rows_at(g, 16), :] = zg[rows_at(g, 16), :]

    group_send(PGB, lambda ry, rc: gated.at[slot_rows, rows_at(ry, 256)], gated_all.at[mine, slot_rows])
    gated_all[mine] = gated[:, rows_at(y, 256)]
    outs[...] = dot(gated[:ROWS, :], w_v[...]).astype(BF)
    local(outs, ho_out, LHO)
    rows32[...] = dot(gated[ROWS:, :], w_v[...])
    for h in range(DP):
        to_v[h] = rows32[2 * h : 2 * h + 2, :].astype(BF)
    local(to_v, to_out, LTO)

    def backward(i):
        rows = slice(TILE * i, TILE * i + TILE)
        count = min(i, 3) + 1
        for j in range(count):
            cols = slice(WIDE * j, WIDE * j + WIDE)
            d_weight = dot_nt(da[rows, :], vst[cols, :])
            dsc[rows, cols] = (d_weight * gst[rows, cols].astype(F32)).astype(BF)
        return (dot(dsc[rows, : WIDE * count], kst[: WIDE * count, :]) * 0.125).astype(BF)

    got(da_raw.at[pl.ds(HIST, 448)], PDT)
    da[HIST:ALL, :] = da_raw[HIST:ALL, :]
    for i in range(4, 6):
        dqt[TILE * (i - 4) : TILE * (i - 3), :] = backward(i)
    seq_send(PQS, lambda p: dqt.at[rows_at(p, SLOTS)], yq.at[rows_at(s, SLOTS)])
    yq[rows_at(s, SLOTS), :] = dqt[rows_at(s, SLOTS), :]

    got(da_raw.at[pl.ds(0, 896)], PDH)
    for i in range(4):
        rows = slice(TILE * i, TILE * i + TILE)
        da[rows, :] = jnp.where(tile_row < length - TILE * i, da_raw[rows, :].astype(F32), 0.0).astype(BF)
    for i in range(4):
        gq[TILE * i : TILE * i + TILE, :] = backward(i)

    def grads_send(phase, buf, base):
        place = dqkvu_out.at[:, pl.ds(pl.multiple_of(base + s * 128, 128), 128)]
        seq_send(phase, lambda p: buf.at[rows_at(p, ROWS)], place)
        local(buf.at[rows_at(s, ROWS)], place, LGR)

    grads_send(PGQ, gq, 2 * D)

    def key_sum(left, right, j):
        both = dot_tn(left[TILE * j : ALL, WIDE * j : WIDE * j + WIDE], right[TILE * j : ALL, :])
        return jnp.where(lane < 64, both[:TILE, :], both[TILE:, :])

    for j in range(4):
        gk[TILE * j : TILE * j + TILE, :] = (key_sum(dsc, qs, j) * 2.0).astype(BF)
    grads_send(PGK, gk, 3 * D)
    for j in range(4):
        gv[TILE * j : TILE * j + TILE, :] = key_sum(wst, da, j).astype(BF)
    grads_send(PGV, gv, D)

    got(yq.at[pl.ds(0, 448)], PQS)
    zq[...] = dot(perm_back, yq[...]).astype(BF)
    dp_send(PQD, zq, rq)
    rq[rows_at(g, 16), :] = zq[rows_at(g, 16), :]

    got(cot_all.at[pl.ds(0, 7)], PCO)
    got(gated_all.at[pl.ds(0, 7), hist_rows], PGA)
    got(gated_all.at[pl.ds(0, 7), slot_rows], PGB)
    y_own[...] = dot_tn(gated_all[...].reshape(8 * 192, 256), cot_all[...].reshape(8 * 192, 512))
    for d in range(1, NZ):
        zp = lax.rem(z + d, NZ)
        z_send[zp] = y_own[rows_at(zp, 32), :].astype(BF)
        send(z_send.at[zp], z_recv.at[z], PZ, {"dp": y * NZ + zp})
    z_own[...] = y_own[rows_at(z, 32), :]

    got(rg.at[pl.ds(0, 496)], PGT)
    got(rq.at[pl.ds(0, 496)], PQD)
    returned = jnp.concatenate([rq[...], rg[...]], axis=1)
    d_items = dot(sel_t[...], returned).astype(BF)
    for k in range(SEQ):
        di[:, 128 * k : 128 * k + 128] = d_items[64 * k : 64 * k + 64, :128]
        di[:, D + 128 * k : D + 128 * k + 128] = d_items[64 * k : 64 * k + 64, 128:]
    local(di, di_out, LDI)

    got(z_recv.at[pl.ds(0, NZ - 1)], PZ)
    total = z_own[...]
    for d in range(1, NZ):
        total = total + z_recv[lax.rem(z + d, NZ)].astype(F32)
    x_send[...] = total
    seq_send(PX, lambda p: x_send.at[rows_at(lax.div(p, 2), 8)], x_recv.at[s])
    x_recv[s] = x_send[rows_at(lax.div(s, 2), 8), :]
    got(x_recv.at[pl.ds(0, SEQ - 1)], PX)
    halves = [x_recv[c] + x_recv[2 + c] + x_recv[4 + c] + x_recv[6 + c] for c in range(2)]
    full = jnp.concatenate(halves, axis=1) * (32768.0 ** -0.5)
    dw[...] = jnp.where(core == 0, full[:4, :], full[4:, :])
    local(dw, dw_out, LDW)

    for phase, buf in ((PGQ, gq), (PGK, gk), (PGV, gv)):
        got(buf.at[pl.ds(0, 896)], phase)
        sent(buf.at[pl.ds(0, 896)], phase)
        local_wait(buf.at[pl.ds(0, ROWS)], LGR)
    for phase, buf in ((PK, kraw), (PQ, qraw), (PV, vraw), (PAH, o_h), (PDH, da_raw)):
        sent(buf.at[pl.ds(0, 896)], phase)
    for phase, buf in ((PTQ, tq), (PAT, o_h), (PDT, da_raw), (PQS, dqt)):
        sent(buf.at[pl.ds(0, 448)], phase)
    for phase, buf in ((PT, tsend), (PGT, zg), (PQD, zq)):
        sent(buf.at[pl.ds(0, 496)], phase)
    sent(cot_all.at[pl.ds(0, 7)], PCO)
    sent(gated_all.at[pl.ds(0, 7), hist_rows], PGA)
    sent(gated_all.at[pl.ds(0, 7), slot_rows], PGB)
    sent(z_send.at[pl.ds(0, NZ - 1)], PZ)
    sent(x_recv.at[pl.ds(0, SEQ - 1)], PX)
    local_wait(du_h, LDU)
    local_wait(outs, LHO)
    local_wait(to_v, LTO)
    local_wait(di, LDI)
    local_wait(dw, LDW)


def deliver(ho, to, dqkvu, di, dw, ho_out, to_out, dqkvu_out, di_out, dw_out, sem):
    pairs = [(dqkvu.at[pl.ds(32 * r, 32)], dqkvu_out.at[pl.ds(32 * r, 32)]) for r in range(4)]
    pairs += [(ho, ho_out), (to, to_out), (di, di_out), (dw, dw_out)]
    copies = [pltpu.make_async_copy(a, b, sem.at[n]) for n, (a, b) in enumerate(pairs)]
    for copy in copies:
        copy.start()
    for copy in copies:
        copy.wait()


def scratch():
    def vm(*shape, dtype=BF):
        return pltpu.VMEM(shape, dtype)

    return [
        vm(HIST, 128), vm(HIST, 128), vm(ALL, 128), vm(ALL, 128),
        vm(2 * HIST, 128), vm(2 * HIST, 128),
        vm(ALL, 2 * HIST), vm(ALL, 2 * HIST), vm(ALL, 2 * HIST),
        vm(2, DP, dtype=jnp.int32), vm(1, DP, dtype=jnp.int32), vm(SLOTS, 2 * D), vm(1, D, dtype=F32),
        vm(ROWS, D), vm(D, D), vm(DP, 2, D), vm(DP, 2, D), vm(SLOTS, D, dtype=F32),
        vm(ROWS + SLOTS, D), vm(ROWS + SLOTS, D, dtype=F32),
        vm(512, 512), vm(512, 256), vm(512, 256), vm(512, 128), vm(SLOTS, D),
        vm(ALL, 128), vm(SEQ, ROWS + SLOTS, 128), vm(SEQ, ROWS + SLOTS, 128),
        vm(ALL, 128), vm(ALL, 128),
        vm(ROWS + SLOTS, D), vm(ROWS, D), vm(ROWS, D), vm(SLOTS, D),
        vm(512, 128), vm(512, 128), vm(512, 128), vm(512, 128), vm(512, 128), vm(512, 128),
        vm(HIST, 128), vm(HIST, 128), vm(HIST, 128), vm(SLOTS, 2 * D),
        vm(8, ROWS + SLOTS, 512), vm(8, ROWS + SLOTS, 256), vm(256, 512, dtype=F32),
        vm(NZ, 32, 512), vm(32, 512, dtype=F32), vm(NZ, 32, 512),
        vm(32, 512, dtype=F32), vm(SEQ, 8, 512, dtype=F32), vm(4, D, dtype=F32),
        pltpu.SemaphoreType.DMA((NPH,)),
        pltpu.SemaphoreType.DMA((NPH,)),
        pltpu.SemaphoreType.DMA((NLOC,)),
    ]


def shards(qkvu, lengths, items, send_list, send_count, w_out, gain, g_hist, g_tgt):
    hbm = pl.BlockSpec(memory_space=pltpu.HBM)
    vmem = pl.BlockSpec(memory_space=pltpu.VMEM)
    results = pl.pallas_call(
        kernel,
        out_shape=(
            pltpu.VMEM((ROWS, D), BF),
            pltpu.VMEM((DP, 2, D), BF),
            pltpu.VMEM((ROWS, 4 * D), BF),
            pltpu.VMEM((SLOTS, 2 * D), BF),
            pltpu.VMEM((4, D), F32),
        ),
        in_specs=[hbm, hbm, pl.BlockSpec(memory_space=pltpu.SMEM)] + [hbm] * 6,
        out_specs=(vmem,) * 5,
        scratch_shapes=scratch(),
        compiler_params=pltpu.CompilerParams(
            collective_id=0, has_side_effects=True, vmem_limit_bytes=56 * 1024 * 1024
        ),
    )(
        send_list[0, 0].T, send_count[0], lengths, qkvu[0], items[0, 0], w_out, gain.reshape(1, D), g_hist[0], g_tgt[0, 0]
    )
    hist_out, tgt_out, d_qkvu, d_items, d_w2 = pl.pallas_call(
        deliver,
        out_shape=tuple(jax.ShapeDtypeStruct(r.shape, r.dtype) for r in results),
        in_specs=(vmem,) * 5,
        out_specs=(hbm,) * 5,
        scratch_shapes=[pltpu.SemaphoreType.DMA((8,))],
        compiler_params=pltpu.CompilerParams(vmem_limit_bytes=8 * 1024 * 1024),
    )(*results)
    return (
        hist_out[None],
        tgt_out[None, None],
        d_qkvu[None],
        d_items[None, None],
        d_w2,
    )


def solution(mesh):
    in_specs = (
        P("dp", "seq", None),
        P("dp"),
        P("dp", "seq", None, None),
        P("dp", "seq", None, None),
        P("dp", "seq", None),
        P(),
        P(),
        P("dp", "seq", None),
        P("dp", "seq", None, None, None),
    )
    out_specs = (
        P("dp", "seq", None),
        P("dp", "seq", None, None, None),
        P("dp", "seq", None),
        P("dp", "seq", None, None),
        P(("dp", "seq"), None),
    )
    return jax.shard_map(shards, mesh=mesh, in_specs=in_specs, out_specs=out_specs, check_vma=False)
```

```python
import jax
import jax.numpy as jnp
from jax import lax
from jax.experimental import pallas as pl
from jax.experimental.pallas import tpu as pltpu
from jax.sharding import PartitionSpec as P

BF = jnp.bfloat16
F32 = jnp.float32
MESH = pl.DeviceIdType.MESH

D = 1024
SEQ = 8
DP = 32
NY = 4
NZ = 8
ROWS = 128
SLOTS = 64
HIST = 1024
ALL = 1536
TILE = 256
WIDE = 2 * TILE

(PK, PQ, PV, PT, PTQ, PAH, PAT, PDH, PDT, PSH, PST, PGT, PQS, PQD, PGQ, PGK, PGV, PCO, PCF, PGA, PGB, PZ, PX, NPH) = range(24)
(LLI, LCO, LIT, LGA, LIN, LW, LCOT, LGT, LU, LHO, LTO, LDU, LGR, LDI, LDW, NLOC) = range(16)


def dot(a, b):
    return lax.dot_general(a, b, (((1,), (0,)), ((), ())), preferred_element_type=F32)


def dot_nt(a, b):
    return lax.dot_general(a, b, (((1,), (1,)), ((), ())), preferred_element_type=F32)


def dot_tn(a, b):
    return lax.dot_general(a, b, (((0,), (0,)), ((), ())), preferred_element_type=F32)


def one_hot(condition):
    return jnp.where(condition, 1.0, 0.0).astype(BF)


def kernel(
    lists_hbm, counts_hbm, length_ref, qkvu, items_hbm, w_hbm, gain_hbm, gh_hbm, gt_hbm,
    ho_out, to_out, dqkvu_out, di_out, dw_out,
    kraw, vraw, qraw, qs, kst, vst, wst, gst, dsc,
    lists, counts, items, gain, u_v, w_v, gt_v, to_v, rows32, cot, dz, sel_t, tsend, trecv, tq, tgate,
    o_h, att_r, datt, da_raw, da, gated, outs, du_h, dgt, zg, rg, dqt, yq, zq, rq,
    gq, gk, gv, di, st_hs, st_ts, st_h, st_t, gated_p, cot_all, gated_all, y_own, z_send, z_recv, x_send, x_recv, dw,
    ssem, rsem, lsem,
):
    g = lax.axis_index("dp")
    s = lax.axis_index("seq")
    y, z = lax.div(g, NZ), lax.rem(g, NZ)
    x = lax.div(s, 2)
    core = lax.rem(s, 2)
    other = s + 1 - 2 * core
    mine = 2 * y + core
    length = length_ref[0]

    def rows_at(index, size):
        return pl.ds(pl.multiple_of(index * size, size), size)

    barrier = pltpu.get_barrier_semaphore()

    def greet_dp(d, carry):
        pl.semaphore_signal(barrier, inc=1, device_id={"dp": lax.rem(g + d, DP)}, device_id_type=MESH)
        return carry

    for d in range(1, SEQ):
        pl.semaphore_signal(barrier, inc=1, device_id={"seq": lax.rem(s + d, SEQ)}, device_id_type=MESH)
    lax.fori_loop(1, DP, greet_dp, 0)
    for d in range(1, NY):
        pl.semaphore_signal(
            barrier, inc=1, device_id={"dp": lax.rem(y + d, NY) * NZ + z, "seq": other}, device_id_type=MESH
        )

    def local(src, dst, sem):
        copy = pltpu.make_async_copy(src, dst, lsem.at[sem])
        copy.start()

    def local_wait(ref, sem):
        pltpu.make_async_copy(ref, ref, lsem.at[sem]).wait()

    def send(src, dst, phase, device):
        pltpu.make_async_remote_copy(
            src_ref=src, dst_ref=dst, send_sem=ssem.at[phase], recv_sem=rsem.at[phase],
            device_id=device, device_id_type=MESH,
        ).start()

    def seq_send(phase, src, dst):
        for d in range(1, SEQ):
            p = lax.rem(s + d, SEQ)
            send(src(p), dst, phase, {"seq": p})

    def got(ref, phase):
        pltpu.make_async_copy(ref, ref, rsem.at[phase]).wait()

    def sent(ref, phase):
        pltpu.make_async_copy(ref, ref, ssem.at[phase]).wait()

    local(lists_hbm, lists, LLI)
    local(counts_hbm, counts, LCO)
    local(items_hbm, items, LIT)
    local(gain_hbm, gain, LGA)
    for base, buf in ((3 * D, kraw), (2 * D, qraw), (D, vraw)):
        local(qkvu.at[:, pl.ds(pl.multiple_of(base + s * 128, 128), 128)], buf.at[rows_at(s, ROWS)], LIN)
    local(w_hbm, w_v, LW)
    local(gh_hbm, cot.at[pl.ds(0, ROWS)], LCOT)
    local(gt_hbm, gt_v, LGT)
    local(qkvu.at[:, pl.ds(0, D)], u_v, LU)

    local_wait(lists, LLI)
    local_wait(counts, LCO)
    lane512 = lax.broadcasted_iota(jnp.int32, (DP, 512), 1)
    spread = one_hot((lane512 >> 4) == lax.broadcasted_iota(jnp.int32, (DP, 512), 0))

    def spread_row(row):
        return dot(jnp.broadcast_to(row.astype(F32), (16, DP)).astype(BF), spread)[:1, :]

    slot = lax.broadcasted_iota(jnp.int32, (1, 512), 1)
    second = (slot & 1) == 1
    picked = jnp.where(second, spread_row(lists[1:2, :]), spread_row(lists[0:1, :]))
    live = spread_row(counts[...]) > jnp.where(second, 1.5, 0.5)
    code = jnp.where(live, picked + (((slot >> 1) & 7) * SLOTS).astype(F32), -1.0)
    sel_t[...] = one_hot(lax.broadcasted_iota(jnp.int32, (512, 512), 0).astype(F32) == code)
    local_wait(items, LIT)
    stacked = jnp.concatenate(
        [
            jnp.concatenate([items[:, 128 * k : 128 * k + 128], items[:, D + 128 * k : D + 128 * k + 128]], axis=1)
            for k in range(SEQ)
        ],
        axis=0,
    )
    tsend[...] = dot_tn(sel_t[...], stacked).astype(BF)

    pl.semaphore_wait(barrier, SEQ - 1 + DP - 1 + NY - 1)

    def dp_send(phase, src, dst):
        def one(d, carry):
            p = lax.rem(g + d, DP)
            send(src.at[rows_at(p, 16)], dst.at[rows_at(g, 16)], phase, {"dp": p})
            return carry

        lax.fori_loop(1, DP, one, 0)

    def columns_send(phase, base, buf):
        seq_send(
            phase, lambda p: qkvu.at[:, pl.ds(pl.multiple_of(base + p * 128, 128), 128)], buf.at[rows_at(s, ROWS)]
        )

    columns_send(PK, 3 * D, kraw)
    dp_send(PT, tsend, trecv)
    columns_send(PQ, 2 * D, qraw)
    columns_send(PV, D, vraw)
    trecv[rows_at(g, 16), :] = tsend[rows_at(g, 16), :]

    local_wait(w_v, LW)
    local_wait(cot.at[pl.ds(0, ROWS)], LCOT)
    local_wait(gt_v, LGT)
    for h in range(DP):
        rows32[2 * h : 2 * h + 2, :] = gt_v[h].astype(F32)
    cot[ROWS:, :] = rows32[...].astype(BF)
    for d in range(1, NY):
        send(cot, cot_all.at[mine], PCO, {"dp": lax.rem(y + d, NY) * NZ + z})
    send(cot, cot_all.at[mine], PCF, {"seq": other})
    dz[...] = dot_nt(cot[...], w_v[...])

    def d_norm(first, gate_ref, gate_first):
        rows = pl.ds(pl.multiple_of(first, 32), 32)
        gate = gate_ref[pl.ds(pl.multiple_of(gate_first, 32), 32), :].astype(F32)
        value = (dz[rows, :] * gain[...] * gate).astype(BF)
        for k in range(SEQ):
            datt[k, rows, :] = value[:, 128 * k : 128 * k + 128]

    def d_norm_hist(r, carry):
        d_norm(r * 32, u_v, r * 32)
        return carry

    def d_norm_tgt(r, carry):
        d_norm(ROWS + r * 32, tgate, r * 32)
        return carry

    target_rows = pl.ds(pl.multiple_of(HIST + s * SLOTS, SLOTS), SLOTS)
    local_wait(u_v, LU)
    local_wait(gain, LGA)
    lax.fori_loop(0, 4, d_norm_hist, 0)
    seq_send(PDH, lambda p: datt.at[p, pl.ds(0, ROWS)], da_raw.at[rows_at(s, ROWS)])
    da_raw[rows_at(s, ROWS), :] = datt[s, pl.ds(0, ROWS), :]

    row512 = lax.broadcasted_iota(jnp.int32, (512, 512), 0)
    col512 = lax.broadcasted_iota(jnp.int32, (512, 512), 1)
    perm = one_hot(col512 == ((row512 & 63) >> 1) * 16 + (row512 >> 6) * 2 + (row512 & 1))
    perm_back = one_hot(row512 == ((col512 & 63) >> 1) * 16 + (col512 >> 6) * 2 + (col512 & 1))

    got(trecv.at[pl.ds(0, 496)], PT)
    arranged = dot(perm, trecv[...]).astype(BF)
    tq[...] = arranged[:, :128]
    for k in range(SEQ):
        tgate[:, 128 * k : 128 * k + 128] = arranged[64 * k : 64 * k + 64, 128:]
    seq_send(PTQ, lambda p: tq.at[rows_at(p, SLOTS)], qraw.at[target_rows])
    qraw[target_rows, :] = tq[rows_at(s, SLOTS), :]

    lax.fori_loop(0, 2, d_norm_tgt, 0)
    seq_send(PDT, lambda p: datt.at[p, pl.ds(ROWS, SLOTS)], da_raw.at[target_rows])
    da_raw[target_rows, :] = datt[s, pl.ds(ROWS, SLOTS), :]
    cot_all[mine] = cot[...]

    def group_send(phase, rows):
        for d in range(1, 2 * NY):
            r = lax.rem(mine + d, 2 * NY)
            send(
                gated_p.at[rows, rows_at(r, 128)], gated_all.at[mine, rows], phase,
                {"dp": lax.div(r, 2) * NZ + z, "seq": s - core + lax.rem(r, 2)},
            )

    for buf in (kraw, qraw, vraw):
        local_wait(buf.at[pl.ds(0, ROWS)], LIN)
    lane = lax.broadcasted_iota(jnp.int32, (TILE, 128), 1)
    tile_row = lax.broadcasted_iota(jnp.int32, (TILE, 128), 0)

    def stack_heads(raw, out):
        for j in range(4):
            block = raw[TILE * j : TILE * j + TILE, :].astype(F32)
            live = tile_row < length - TILE * j
            out[WIDE * j : WIDE * j + TILE, :] = jnp.where(live & (lane < 64), block, 0.0).astype(BF)
            out[WIDE * j + TILE : WIDE * j + WIDE, :] = jnp.where(live & (lane >= 64), block, 0.0).astype(BF)

    got(kraw.at[pl.ds(0, 896)], PK)
    stack_heads(kraw, kst)
    got(qraw.at[pl.ds(0, 896)], PQ)
    for i in range(4):
        block = qraw[TILE * i : TILE * i + TILE, :].astype(F32) * 0.0625
        qs[TILE * i : TILE * i + TILE, :] = jnp.where(tile_row < length - TILE * i, block, 0.0).astype(BF)

    causal = (lax.broadcasted_iota(jnp.int32, (TILE, WIDE), 1) & (TILE - 1)) <= lax.broadcasted_iota(
        jnp.int32, (TILE, WIDE), 0
    )

    def scores(i):
        rows = slice(TILE * i, TILE * i + TILE)
        count = min(i, 3) + 1
        for j in range(count):
            cols = slice(WIDE * j, WIDE * j + WIDE)
            half = dot_nt(qs[rows, :], kst[cols, :])
            twice = 1.0 + jnp.tanh(half)
            weight = half * twice
            slope = 0.5 * twice * (1.0 - weight) + weight
            if i == j:
                weight = jnp.where(causal, weight, 0.0)
                slope = jnp.where(causal, slope, 0.0)
            wst[rows, cols] = weight.astype(BF)
            gst[rows, cols] = slope.astype(BF)

    def attend(i):
        rows = slice(TILE * i, TILE * i + TILE)
        count = min(i, 3) + 1
        o_h[rows, :] = dot(wst[rows, : WIDE * count], vst[: WIDE * count, :]).astype(BF)

    for i in range(4):
        scores(i)
    got(vraw.at[pl.ds(0, 896)], PV)
    stack_heads(vraw, vst)
    for i in range(4):
        attend(i)

    ones = jnp.ones((128, 128), BF)
    stat_row = lax.broadcasted_iota(jnp.int32, (16, 128), 0)

    def two(value):
        high = value.astype(BF)
        return high, (value - high.astype(F32)).astype(BF)

    def stats(i, base):
        rows = slice(TILE * i, TILE * i + TILE)
        att, dn = o_h[rows, :], da_raw[rows, :]
        centred = att.astype(F32) - dot(att, ones) * (1.0 / 128.0)
        parts = [(0, att), (2, dn)]
        parts += [(1, part) for part in two(centred * centred)]
        parts += [(3, part) for part in two(centred * dn.astype(F32))]
        total = dot_nt(one_hot(stat_row == base + parts[0][0]), parts[0][1])
        for q, part in parts[1:]:
            total = total + dot_nt(one_hot(stat_row == base + q), part)
        return total[:8, :]

    got(da_raw.at[pl.ds(0, 896)], PDH)
    st_hs[:, :TILE] = stats(0, 0) + stats(2, 4)
    st_hs[:, TILE:] = stats(1, 0) + stats(3, 4)
    seq_send(PSH, lambda p: st_hs, st_h.at[s])
    st_h[s] = st_hs[...]
    seq_send(PAH, lambda p: o_h.at[rows_at(p, ROWS)], att_r.at[s, pl.ds(0, ROWS)])
    att_r[s, pl.ds(0, ROWS), :] = o_h[rows_at(s, ROWS), :]

    got(qraw.at[pl.ds(HIST, 448)], PTQ)
    for i in range(4, 6):
        rows = slice(TILE * i, TILE * i + TILE)
        qs[rows, :] = (qraw[rows, :].astype(F32) * 0.0625).astype(BF)
        scores(i)
        attend(i)
    got(da_raw.at[pl.ds(HIST, 448)], PDT)
    st_ts[...] = stats(4, 0) + stats(5, 4)
    seq_send(PST, lambda p: st_ts, st_t.at[s])
    st_t[s] = st_ts[...]
    seq_send(
        PAT,
        lambda p: o_h.at[pl.ds(pl.multiple_of(HIST + p * SLOTS, SLOTS), SLOTS)],
        att_r.at[s, pl.ds(ROWS, SLOTS)],
    )
    att_r[s, pl.ds(ROWS, SLOTS), :] = o_h[target_rows, :]

    def row_terms(received):
        blocks = [received[k] for k in range(SEQ)]
        total = blocks[0]
        for block in blocks[1:]:
            total = total + block
        terms = []
        for base in (0, 4):
            mean = total[base : base + 1] * (1.0 / D)
            squares, product = total[base + 1 : base + 2], total[base + 3 : base + 4]
            for block in blocks:
                shift = block[base : base + 1] * (1.0 / 128.0) - mean
                squares = squares + 128.0 * shift * shift
                product = product + block[base + 2 : base + 3] * shift
            inverse = lax.rsqrt(squares * (1.0 / D) + 1e-05)
            offset = inverse * total[base + 2 : base + 3] * (1.0 / D)
            slope = inverse * inverse * (inverse * product * (1.0 / D))
            zero = jnp.zeros_like(mean)
            terms.append(jnp.concatenate([inverse, offset, slope, mean, zero, zero, zero, zero], axis=0))
        return terms

    spread4 = jnp.where(
        (lax.broadcasted_iota(jnp.int32, (8, 512), 1) >> 7) == lax.broadcasted_iota(jnp.int32, (8, 512), 0), 1.0, 0.0
    )

    def d_attended(i, terms):
        rows = slice(TILE * i, TILE * i + TILE)
        wide = lax.dot_general(
            terms, spread4, (((0,), (0,)), ((), ())), precision=lax.Precision.HIGHEST, preferred_element_type=F32
        )
        value = (
            wide[:, :128] * da_raw[rows, :].astype(F32)
            - wide[:, 128:256]
            - wide[:, 256:384] * (o_h[rows, :].astype(F32) - wide[:, 384:])
        )
        if i < 4:
            value = jnp.where(tile_row < length - TILE * i, value, 0.0)
        da[rows, :] = value.astype(BF)

    def backward(i):
        rows = slice(TILE * i, TILE * i + TILE)
        count = min(i, 3) + 1
        for j in range(count):
            cols = slice(WIDE * j, WIDE * j + WIDE)
            d_weight = dot_nt(da[rows, :], vst[cols, :])
            dsc[rows, cols] = (d_weight * gst[rows, cols].astype(F32)).astype(BF)
        return (dot(dsc[rows, : WIDE * count], kst[: WIDE * count, :]) * 0.125).astype(BF)

    def grads_send(phase, buf, base):
        place = dqkvu_out.at[:, pl.ds(pl.multiple_of(base + s * 128, 128), 128)]
        seq_send(phase, lambda p: buf.at[rows_at(p, ROWS)], place)
        local(buf.at[rows_at(s, ROWS)], place, LGR)

    got(st_h.at[pl.ds(0, SEQ - 1)], PSH)
    lower, upper = row_terms(st_h)
    for i in range(4):
        d_attended(i, (lower, upper)[i // 2][:, TILE * (i % 2) : TILE * (i % 2) + TILE])
    for i in range(4):
        gq[TILE * i : TILE * i + TILE, :] = backward(i)
    grads_send(PGQ, gq, 2 * D)

    row256 = lax.broadcasted_iota(jnp.int32, (TILE, TILE), 0)
    col256 = lax.broadcasted_iota(jnp.int32, (TILE, TILE), 1)
    perm_core = one_hot(row256 == ((col256 & 127) >> 2) * 8 + (col256 >> 7) * 4 + (col256 & 3))

    def reorder(rows):
        for k in range(NY):
            cols = slice(TILE * k, TILE * k + TILE)
            gated_p[rows, cols] = dot(gated[rows, cols], perm_core).astype(BF)

    def norm(first, gate_ref, gate_first, du_ref):
        rows = pl.ds(pl.multiple_of(first, 32), 32)
        gate_rows = pl.ds(pl.multiple_of(gate_first, 32), 32)
        att = jnp.concatenate([att_r[k, rows, :] for k in range(SEQ)], axis=1).astype(F32)
        centred = att - jnp.mean(att, axis=1, keepdims=True)
        inverse = lax.rsqrt(jnp.mean(centred * centred, axis=1, keepdims=True) + 1e-05)
        normed = centred * inverse
        gate = gate_ref[gate_rows, :].astype(F32)
        gated[rows, :] = (normed * gain[...] * gate).astype(BF)
        scaled = dz[rows, :] * gain[...]
        du_ref[gate_rows, :] = (scaled * normed).astype(BF)

    def norm_hist(r, carry):
        norm(r * 32, u_v, r * 32, du_h)
        return carry

    def norm_tgt(r, carry):
        norm(ROWS + r * 32, tgate, r * 32, dgt)
        return carry

    got(att_r.at[pl.ds(0, 7), pl.ds(0, ROWS)], PAH)
    lax.fori_loop(0, 4, norm_hist, 0)
    local(du_h, dqkvu_out.at[:, pl.ds(0, D)], LDU)
    hist_rows = pl.ds(0, ROWS)
    slot_rows = pl.ds(ROWS, SLOTS)
    reorder(slice(0, ROWS))
    group_send(PGA, hist_rows)

    got(att_r.at[pl.ds(0, 7), pl.ds(ROWS, SLOTS)], PAT)
    lax.fori_loop(0, 2, norm_tgt, 0)
    reorder(slice(ROWS, ROWS + SLOTS))
    group_send(PGB, slot_rows)
    gated_all[mine] = gated_p[:, rows_at(mine, 128)]

    gate_stack = jnp.concatenate([dgt[:, 128 * k : 128 * k + 128] for k in range(SEQ)], axis=0)
    zg[...] = dot(perm_back, gate_stack).astype(BF)
    dp_send(PGT, zg, rg)
    rg[rows_at(g, 16), :] = zg[rows_at(g, 16), :]

    got(cot_all.at[pl.ds(0, NY - 1)], PCO)
    for d in range(1, NY):
        place = cot_all.at[2 * lax.rem(y + d, NY) + core]
        send(place, place, PCF, {"seq": other})

    got(st_t.at[pl.ds(0, SEQ - 1)], PST)
    for i, terms in enumerate(row_terms(st_t)):
        d_attended(4 + i, terms)
    for i in range(4, 6):
        dqt[TILE * (i - 4) : TILE * (i - 3), :] = backward(i)
    seq_send(PQS, lambda p: dqt.at[rows_at(p, SLOTS)], yq.at[rows_at(s, SLOTS)])
    yq[rows_at(s, SLOTS), :] = dqt[rows_at(s, SLOTS), :]

    def key_sum(left, right, j):
        both = dot_tn(left[TILE * j : ALL, WIDE * j : WIDE * j + WIDE], right[TILE * j : ALL, :])
        return jnp.where(lane < 64, both[:TILE, :], both[TILE:, :])

    for j in range(4):
        gk[TILE * j : TILE * j + TILE, :] = (key_sum(dsc, qs, j) * 2.0).astype(BF)
    grads_send(PGK, gk, 3 * D)
    for j in range(4):
        gv[TILE * j : TILE * j + TILE, :] = key_sum(wst, da, j).astype(BF)
    grads_send(PGV, gv, D)

    got(cot_all.at[pl.ds(0, NY)], PCF)
    got(gated_all.at[pl.ds(0, 7), hist_rows], PGA)
    got(gated_all.at[pl.ds(0, 7), slot_rows], PGB)
    y_own[...] = dot_tn(gated_all[...].reshape(8 * 192, 128), cot_all[...].reshape(8 * 192, D))
    for d in range(1, NZ):
        zp = lax.rem(z + d, NZ)
        z_send[zp] = y_own[rows_at(zp, 16), :].astype(BF)
        send(z_send.at[zp], z_recv.at[z], PZ, {"dp": y * NZ + zp})

    got(yq.at[pl.ds(0, 448)], PQS)
    zq[...] = dot(perm_back, yq[...]).astype(BF)
    dp_send(PQD, zq, rq)
    rq[rows_at(g, 16), :] = zq[rows_at(g, 16), :]

    outs[...] = dot(gated[:ROWS, :], w_v[...]).astype(BF)
    local(outs, ho_out, LHO)
    rows32[...] = dot(gated[ROWS:, :], w_v[...])
    for h in range(DP):
        to_v[h] = rows32[2 * h : 2 * h + 2, :].astype(BF)
    local(to_v, to_out, LTO)

    got(z_recv.at[pl.ds(0, NZ - 1)], PZ)
    total = y_own[rows_at(z, 16), :]
    for d in range(1, NZ):
        total = total + z_recv[lax.rem(z + d, NZ)].astype(F32)
    for q in range(4):
        rows = total[4 * q : 4 * q + 4, :]
        x_send[q] = jnp.concatenate([rows[:, :512], rows[:, 512:]], axis=0)
    for d in range(1, 4):
        xp = lax.rem(x + d, 4)
        send(x_send.at[xp], x_recv.at[x], PX, {"seq": 2 * xp + core})
    x_recv[x] = x_send[x]

    got(rg.at[pl.ds(0, 496)], PGT)
    got(rq.at[pl.ds(0, 496)], PQD)
    returned = jnp.concatenate([rq[...], rg[...]], axis=1)
    d_items = dot(sel_t[...], returned).astype(BF)
    for k in range(SEQ):
        di[:, 128 * k : 128 * k + 128] = d_items[64 * k : 64 * k + 64, :128]
        di[:, D + 128 * k : D + 128 * k + 128] = d_items[64 * k : 64 * k + 64, 128:]
    local(di, di_out, LDI)

    got(x_recv.at[pl.ds(0, 3)], PX)
    full = (x_recv[0] + x_recv[1] + x_recv[2] + x_recv[3]) * (32768.0 ** -0.5)
    dw[...] = jnp.concatenate([full[:4, :], full[4:, :]], axis=1)
    local(dw, dw_out, LDW)

    for phase, buf in ((PGQ, gq), (PGK, gk), (PGV, gv)):
        got(buf.at[pl.ds(0, 896)], phase)
        sent(buf.at[pl.ds(0, 896)], phase)
        local_wait(buf.at[pl.ds(0, ROWS)], LGR)
    for phase, buf in ((PK, kraw), (PQ, qraw), (PV, vraw), (PAH, o_h), (PDH, da_raw)):
        sent(buf.at[pl.ds(0, 896)], phase)
    for phase, buf in ((PTQ, tq), (PAT, o_h), (PDT, da_raw), (PQS, dqt)):
        sent(buf.at[pl.ds(0, 448)], phase)
    for phase, buf in ((PT, tsend), (PGT, zg), (PQD, zq)):
        sent(buf.at[pl.ds(0, 496)], phase)
    sent(cot_all.at[pl.ds(0, NY - 1)], PCO)
    sent(cot_all.at[pl.ds(0, NY)], PCF)
    sent(st_h.at[pl.ds(0, SEQ - 1)], PSH)
    sent(st_t.at[pl.ds(0, SEQ - 1)], PST)
    sent(gated_all.at[pl.ds(0, 7), hist_rows], PGA)
    sent(gated_all.at[pl.ds(0, 7), slot_rows], PGB)
    sent(z_send.at[pl.ds(0, NZ - 1)], PZ)
    sent(x_recv.at[pl.ds(0, 3)], PX)
    local_wait(du_h, LDU)
    local_wait(outs, LHO)
    local_wait(to_v, LTO)
    local_wait(di, LDI)
    local_wait(dw, LDW)


def deliver(ho, to, dqkvu, di, dw, ho_out, to_out, dqkvu_out, di_out, dw_out, sem):
    pairs = [(dqkvu.at[pl.ds(32 * r, 32)], dqkvu_out.at[pl.ds(32 * r, 32)]) for r in range(4)]
    pairs += [(ho, ho_out), (to, to_out), (di, di_out), (dw, dw_out)]
    copies = [pltpu.make_async_copy(a, b, sem.at[n]) for n, (a, b) in enumerate(pairs)]
    for copy in copies:
        copy.start()
    for copy in copies:
        copy.wait()


def scratch():
    def vm(*shape, dtype=BF):
        return pltpu.VMEM(shape, dtype)

    return [
        vm(HIST, 128), vm(HIST, 128), vm(ALL, 128), vm(ALL, 128),
        vm(2 * HIST, 128), vm(2 * HIST, 128),
        vm(ALL, 2 * HIST), vm(ALL, 2 * HIST), vm(ALL, 2 * HIST),
        vm(2, DP, dtype=jnp.int32), vm(1, DP, dtype=jnp.int32), vm(SLOTS, 2 * D), vm(1, D, dtype=F32),
        vm(ROWS, D), vm(D, D), vm(DP, 2, D), vm(DP, 2, D), vm(SLOTS, D, dtype=F32),
        vm(ROWS + SLOTS, D), vm(ROWS + SLOTS, D, dtype=F32),
        vm(512, 512), vm(512, 256), vm(512, 256), vm(512, 128), vm(SLOTS, D),
        vm(ALL, 128), vm(SEQ, ROWS + SLOTS, 128), vm(SEQ, ROWS + SLOTS, 128),
        vm(ALL, 128), vm(ALL, 128),
        vm(ROWS + SLOTS, D), vm(ROWS, D), vm(ROWS, D), vm(SLOTS, D),
        vm(512, 128), vm(512, 128), vm(512, 128), vm(512, 128), vm(512, 128), vm(512, 128),
        vm(HIST, 128), vm(HIST, 128), vm(HIST, 128), vm(SLOTS, 2 * D),
        vm(8, 512, dtype=F32), vm(8, TILE, dtype=F32),
        vm(SEQ, 8, 512, dtype=F32), vm(SEQ, 8, TILE, dtype=F32),
        vm(ROWS + SLOTS, D), vm(8, ROWS + SLOTS, D), vm(8, ROWS + SLOTS, 128),
        vm(128, D, dtype=F32), vm(NZ, 16, D), vm(NZ, 16, D),
        vm(4, 8, 512, dtype=F32), vm(4, 8, 512, dtype=F32), vm(4, D, dtype=F32),
        pltpu.SemaphoreType.DMA((NPH,)),
        pltpu.SemaphoreType.DMA((NPH,)),
        pltpu.SemaphoreType.DMA((NLOC,)),
    ]


def shards(qkvu, lengths, items, send_list, send_count, w_out, gain, g_hist, g_tgt):
    hbm = pl.BlockSpec(memory_space=pltpu.HBM)
    vmem = pl.BlockSpec(memory_space=pltpu.VMEM)
    results = pl.pallas_call(
        kernel,
        out_shape=(
            pltpu.VMEM((ROWS, D), BF),
            pltpu.VMEM((DP, 2, D), BF),
            pltpu.VMEM((ROWS, 4 * D), BF),
            pltpu.VMEM((SLOTS, 2 * D), BF),
            pltpu.VMEM((4, D), F32),
        ),
        in_specs=[hbm, hbm, pl.BlockSpec(memory_space=pltpu.SMEM)] + [hbm] * 6,
        out_specs=(vmem,) * 5,
        scratch_shapes=scratch(),
        compiler_params=pltpu.CompilerParams(
            collective_id=0, has_side_effects=True, vmem_limit_bytes=56 * 1024 * 1024
        ),
    )(
        send_list[0, 0].T, send_count[0], lengths, qkvu[0], items[0, 0], w_out, gain.reshape(1, D), g_hist[0], g_tgt[0, 0]
    )
    hist_out, tgt_out, d_qkvu, d_items, d_w2 = pl.pallas_call(
        deliver,
        out_shape=tuple(jax.ShapeDtypeStruct(r.shape, r.dtype) for r in results),
        in_specs=(vmem,) * 5,
        out_specs=(hbm,) * 5,
        scratch_shapes=[pltpu.SemaphoreType.DMA((8,))],
        compiler_params=pltpu.CompilerParams(vmem_limit_bytes=8 * 1024 * 1024),
    )(*results)
    return (
        hist_out[None],
        tgt_out[None, None],
        d_qkvu[None],
        d_items[None, None],
        d_w2,
    )


def solution(mesh):
    in_specs = (
        P("dp", "seq", None),
        P("dp"),
        P("dp", "seq", None, None),
        P("dp", "seq", None, None),
        P("dp", "seq", None),
        P(),
        P(),
        P("dp", "seq", None),
        P("dp", "seq", None, None, None),
    )
    out_specs = (
        P("dp", "seq", None),
        P("dp", "seq", None, None, None),
        P("dp", "seq", None),
        P("dp", "seq", None, None),
        P(("dp", "seq"), None),
    )
    return jax.shard_map(shards, mesh=mesh, in_specs=in_specs, out_specs=out_specs, check_vma=False)
```

```python
import jax
import jax.numpy as jnp
from jax import lax
from jax.experimental import pallas as pl
from jax.experimental.pallas import tpu as pltpu
from jax.sharding import PartitionSpec as P

BF = jnp.bfloat16
F32 = jnp.float32
MESH = pl.DeviceIdType.MESH

D = 1024
SEQ = 8
DP = 32
NY = 4
NZ = 8
ROWS = 128
SLOTS = 64
HIST = 1024
ALL = 1536
TILE = 256
WIDE = 2 * TILE

(PK, PQ, PV, PT, PTQ, PAH, PAT, PDH, PDT, PSH, PST, PGT, PQS, PQD, PGQ, PGK, PGV, PCO, PCF, PGA, PGB, PZ, PX, NPH) = range(24)
(LLI, LCO, LIT, LGA, LIN, LW, LCOT, LGT, LU, LHO, LTO, LDU, LGR, LDI, LDW, NLOC) = range(16)


def dot(a, b):
    return lax.dot_general(a, b, (((1,), (0,)), ((), ())), preferred_element_type=F32)


def dot_nt(a, b):
    return lax.dot_general(a, b, (((1,), (1,)), ((), ())), preferred_element_type=F32)


def dot_tn(a, b):
    return lax.dot_general(a, b, (((0,), (0,)), ((), ())), preferred_element_type=F32)


def one_hot(condition):
    return jnp.where(condition, 1.0, 0.0).astype(BF)


def kernel(
    lists_hbm, counts_hbm, length_ref, qkvu, items_hbm, w_hbm, gain_hbm, gh_hbm, gt_hbm,
    ho_out, to_out, dqkvu_out, di_out, dw_out,
    kraw, vraw, qraw, qs, kst, vst, wst, gst, dsc,
    lists, counts, items, gain, u_v, w_v, gt_v, to_v, rows32, cot, dz, sel_t, tsend, trecv, tq, tgate,
    o_h, att_r, datt, da_raw, da, gated, outs, du_h, dgt, zg, rg, dqt, yq, zq, rq,
    gq, gk, gv, di, st_hs, st_ts, st_h, st_t, gated_p, cot_all, gated_all, y_own, z_send, z_recv, x_send, x_recv, dw,
    ssem, rsem, lsem,
):
    g = lax.axis_index("dp")
    s = lax.axis_index("seq")
    y, z = lax.div(g, NZ), lax.rem(g, NZ)
    x = lax.div(s, 2)
    core = lax.rem(s, 2)
    other = s + 1 - 2 * core
    mine = 2 * y + core
    length = length_ref[0]

    def rows_at(index, size):
        return pl.ds(pl.multiple_of(index * size, size), size)

    barrier = pltpu.get_barrier_semaphore()

    def greet_dp(d, carry):
        pl.semaphore_signal(barrier, inc=1, device_id={"dp": lax.rem(g + d, DP)}, device_id_type=MESH)
        return carry

    for d in range(1, SEQ):
        pl.semaphore_signal(barrier, inc=1, device_id={"seq": lax.rem(s + d, SEQ)}, device_id_type=MESH)
    lax.fori_loop(1, DP, greet_dp, 0)
    for d in range(1, NY):
        pl.semaphore_signal(
            barrier, inc=1, device_id={"dp": lax.rem(y + d, NY) * NZ + z, "seq": other}, device_id_type=MESH
        )

    def local(src, dst, sem):
        copy = pltpu.make_async_copy(src, dst, lsem.at[sem])
        copy.start()

    def local_wait(ref, sem):
        pltpu.make_async_copy(ref, ref, lsem.at[sem]).wait()

    def send(src, dst, phase, device):
        pltpu.make_async_remote_copy(
            src_ref=src, dst_ref=dst, send_sem=ssem.at[phase], recv_sem=rsem.at[phase],
            device_id=device, device_id_type=MESH,
        ).start()

    def seq_send(phase, src, dst):
        for d in range(1, SEQ):
            p = lax.rem(s + d, SEQ)
            send(src(p), dst, phase, {"seq": p})

    def got(ref, phase):
        pltpu.make_async_copy(ref, ref, rsem.at[phase]).wait()

    def sent(ref, phase):
        pltpu.make_async_copy(ref, ref, ssem.at[phase]).wait()

    local(lists_hbm, lists, LLI)
    local(counts_hbm, counts, LCO)
    local(items_hbm, items, LIT)
    local(gain_hbm, gain, LGA)
    for base, buf in ((3 * D, kraw), (2 * D, qraw), (D, vraw)):
        local(qkvu.at[:, pl.ds(pl.multiple_of(base + s * 128, 128), 128)], buf.at[rows_at(s, ROWS)], LIN)
    local(w_hbm, w_v, LW)
    local(gh_hbm, cot.at[pl.ds(0, ROWS)], LCOT)
    local(gt_hbm, gt_v, LGT)
    local(qkvu.at[:, pl.ds(0, D)], u_v, LU)

    local_wait(lists, LLI)
    local_wait(counts, LCO)
    lane512 = lax.broadcasted_iota(jnp.int32, (DP, 512), 1)
    spread = one_hot((lane512 >> 4) == lax.broadcasted_iota(jnp.int32, (DP, 512), 0))

    def spread_row(row):
        return dot(jnp.broadcast_to(row.astype(F32), (16, DP)).astype(BF), spread)[:1, :]

    slot = lax.broadcasted_iota(jnp.int32, (1, 512), 1)
    second = (slot & 1) == 1
    picked = jnp.where(second, spread_row(lists[1:2, :]), spread_row(lists[0:1, :]))
    live = spread_row(counts[...]) > jnp.where(second, 1.5, 0.5)
    code = jnp.where(live, picked + (((slot >> 1) & 7) * SLOTS).astype(F32), -1.0)
    sel_t[...] = one_hot(lax.broadcasted_iota(jnp.int32, (512, 512), 0).astype(F32) == code)
    local_wait(items, LIT)
    stacked = jnp.concatenate(
        [
            jnp.concatenate([items[:, 128 * k : 128 * k + 128], items[:, D + 128 * k : D + 128 * k + 128]], axis=1)
            for k in range(SEQ)
        ],
        axis=0,
    )
    tsend[...] = dot_tn(sel_t[...], stacked).astype(BF)

    pl.semaphore_wait(barrier, SEQ - 1 + DP - 1 + NY - 1)

    def dp_send(phase, src, dst):
        def one(d, carry):
            p = lax.rem(g + d, DP)
            send(src.at[rows_at(p, 16)], dst.at[rows_at(g, 16)], phase, {"dp": p})
            return carry

        lax.fori_loop(1, DP, one, 0)

    def columns_send(phase, base, buf):
        seq_send(
            phase, lambda p: qkvu.at[:, pl.ds(pl.multiple_of(base + p * 128, 128), 128)], buf.at[rows_at(s, ROWS)]
        )

    columns_send(PK, 3 * D, kraw)
    dp_send(PT, tsend, trecv)
    columns_send(PQ, 2 * D, qraw)
    columns_send(PV, D, vraw)
    trecv[rows_at(g, 16), :] = tsend[rows_at(g, 16), :]

    local_wait(w_v, LW)
    local_wait(cot.at[pl.ds(0, ROWS)], LCOT)
    local_wait(gt_v, LGT)
    for h in range(DP):
        rows32[2 * h : 2 * h + 2, :] = gt_v[h].astype(F32)
    cot[ROWS:, :] = rows32[...].astype(BF)
    for d in range(1, NY):
        send(cot, cot_all.at[mine], PCO, {"dp": lax.rem(y + d, NY) * NZ + z})
    send(cot, cot_all.at[mine], PCF, {"seq": other})
    dz[...] = dot_nt(cot[...], w_v[...])

    def d_norm(first, gate_ref, gate_first):
        rows = pl.ds(pl.multiple_of(first, 32), 32)
        gate = gate_ref[pl.ds(pl.multiple_of(gate_first, 32), 32), :].astype(F32)
        value = (dz[rows, :] * gain[...] * gate).astype(BF)
        for k in range(SEQ):
            datt[k, rows, :] = value[:, 128 * k : 128 * k + 128]

    def d_norm_hist(r, carry):
        d_norm(r * 32, u_v, r * 32)
        return carry

    def d_norm_tgt(r, carry):
        d_norm(ROWS + r * 32, tgate, r * 32)
        return carry

    target_rows = pl.ds(pl.multiple_of(HIST + s * SLOTS, SLOTS), SLOTS)
    local_wait(u_v, LU)
    local_wait(gain, LGA)
    lax.fori_loop(0, 4, d_norm_hist, 0)
    seq_send(PDH, lambda p: datt.at[p, pl.ds(0, ROWS)], da_raw.at[rows_at(s, ROWS)])
    da_raw[rows_at(s, ROWS), :] = datt[s, pl.ds(0, ROWS), :]

    row512 = lax.broadcasted_iota(jnp.int32, (512, 512), 0)
    col512 = lax.broadcasted_iota(jnp.int32, (512, 512), 1)
    perm = one_hot(col512 == ((row512 & 63) >> 1) * 16 + (row512 >> 6) * 2 + (row512 & 1))
    perm_back = one_hot(row512 == ((col512 & 63) >> 1) * 16 + (col512 >> 6) * 2 + (col512 & 1))

    got(trecv.at[pl.ds(0, 496)], PT)
    arranged = dot(perm, trecv[...]).astype(BF)
    tq[...] = arranged[:, :128]
    for k in range(SEQ):
        tgate[:, 128 * k : 128 * k + 128] = arranged[64 * k : 64 * k + 64, 128:]
    seq_send(PTQ, lambda p: tq.at[rows_at(p, SLOTS)], qraw.at[target_rows])
    qraw[target_rows, :] = tq[rows_at(s, SLOTS), :]

    lax.fori_loop(0, 2, d_norm_tgt, 0)
    seq_send(PDT, lambda p: datt.at[p, pl.ds(ROWS, SLOTS)], da_raw.at[target_rows])
    da_raw[target_rows, :] = datt[s, pl.ds(ROWS, SLOTS), :]
    cot_all[mine] = cot[...]

    def group_send(phase, rows):
        for d in range(1, 2 * NY):
            r = lax.rem(mine + d, 2 * NY)
            send(
                gated_p.at[rows, rows_at(r, 128)], gated_all.at[mine, rows], phase,
                {"dp": lax.div(r, 2) * NZ + z, "seq": s - core + lax.rem(r, 2)},
            )

    for buf in (kraw, qraw, vraw):
        local_wait(buf.at[pl.ds(0, ROWS)], LIN)
    lane = lax.broadcasted_iota(jnp.int32, (TILE, 128), 1)
    tile_row = lax.broadcasted_iota(jnp.int32, (TILE, 128), 0)

    def stack_heads(raw, out):
        for j in range(4):
            block = raw[TILE * j : TILE * j + TILE, :].astype(F32)
            live = tile_row < length - TILE * j
            out[WIDE * j : WIDE * j + TILE, :] = jnp.where(live & (lane < 64), block, 0.0).astype(BF)
            out[WIDE * j + TILE : WIDE * j + WIDE, :] = jnp.where(live & (lane >= 64), block, 0.0).astype(BF)

    got(kraw.at[pl.ds(0, 896)], PK)
    stack_heads(kraw, kst)
    got(qraw.at[pl.ds(0, 896)], PQ)
    for i in range(4):
        block = qraw[TILE * i : TILE * i + TILE, :].astype(F32) * 0.0625
        qs[TILE * i : TILE * i + TILE, :] = jnp.where(tile_row < length - TILE * i, block, 0.0).astype(BF)

    causal = (lax.broadcasted_iota(jnp.int32, (TILE, WIDE), 1) & (TILE - 1)) <= lax.broadcasted_iota(
        jnp.int32, (TILE, WIDE), 0
    )

    def scores(i):
        rows = slice(TILE * i, TILE * i + TILE)
        count = min(i, 3) + 1
        for j in range(count):
            cols = slice(WIDE * j, WIDE * j + WIDE)
            half = dot_nt(qs[rows, :], kst[cols, :])
            twice = 1.0 + jnp.tanh(half)
            weight = half * twice
            slope = 0.5 * twice * (1.0 - weight) + weight
            if i == j:
                weight = jnp.where(causal, weight, 0.0)
                slope = jnp.where(causal, slope, 0.0)
            wst[rows, cols] = weight.astype(BF)
            gst[rows, cols] = slope.astype(BF)

    def attend(i):
        rows = slice(TILE * i, TILE * i + TILE)
        count = min(i, 3) + 1
        o_h[rows, :] = dot(wst[rows, : WIDE * count], vst[: WIDE * count, :]).astype(BF)

    for i in range(4):
        scores(i)
    got(vraw.at[pl.ds(0, 896)], PV)
    stack_heads(vraw, vst)
    for i in range(4):
        attend(i)

    ones = jnp.ones((128, 128), BF)
    stat_row = lax.broadcasted_iota(jnp.int32, (16, 128), 0)

    def two(value):
        high = value.astype(BF)
        return high, (value - high.astype(F32)).astype(BF)

    def stats(i, base):
        rows = slice(TILE * i, TILE * i + TILE)
        att, dn = o_h[rows, :], da_raw[rows, :]
        centred = att.astype(F32) - dot(att, ones) * (1.0 / 128.0)
        parts = [(0, att), (2, dn)]
        parts += [(1, part) for part in two(centred * centred)]
        parts += [(3, part) for part in two(centred * dn.astype(F32))]
        total = dot_nt(one_hot(stat_row == base + parts[0][0]), parts[0][1])
        for q, part in parts[1:]:
            total = total + dot_nt(one_hot(stat_row == base + q), part)
        return total[:8, :]

    got(da_raw.at[pl.ds(0, 896)], PDH)
    st_hs[:, :TILE] = stats(0, 0) + stats(2, 4)
    st_hs[:, TILE:] = stats(1, 0) + stats(3, 4)
    seq_send(PSH, lambda p: st_hs, st_h.at[s])
    st_h[s] = st_hs[...]
    seq_send(PAH, lambda p: o_h.at[rows_at(p, ROWS)], att_r.at[s, pl.ds(0, ROWS)])
    att_r[s, pl.ds(0, ROWS), :] = o_h[rows_at(s, ROWS), :]

    got(qraw.at[pl.ds(HIST, 448)], PTQ)
    for i in range(4, 6):
        rows = slice(TILE * i, TILE * i + TILE)
        qs[rows, :] = (qraw[rows, :].astype(F32) * 0.0625).astype(BF)
        scores(i)
        attend(i)
    seq_send(
        PAT,
        lambda p: o_h.at[pl.ds(pl.multiple_of(HIST + p * SLOTS, SLOTS), SLOTS)],
        att_r.at[s, pl.ds(ROWS, SLOTS)],
    )
    got(da_raw.at[pl.ds(HIST, 448)], PDT)
    st_ts[...] = stats(4, 0) + stats(5, 4)
    seq_send(PST, lambda p: st_ts, st_t.at[s])
    st_t[s] = st_ts[...]
    att_r[s, pl.ds(ROWS, SLOTS), :] = o_h[target_rows, :]

    def row_terms(received):
        blocks = [received[k] for k in range(SEQ)]
        total = blocks[0]
        for block in blocks[1:]:
            total = total + block
        terms = []
        for base in (0, 4):
            mean = total[base : base + 1] * (1.0 / D)
            squares, product = total[base + 1 : base + 2], total[base + 3 : base + 4]
            for block in blocks:
                shift = block[base : base + 1] * (1.0 / 128.0) - mean
                squares = squares + 128.0 * shift * shift
                product = product + block[base + 2 : base + 3] * shift
            inverse = lax.rsqrt(squares * (1.0 / D) + 1e-05)
            offset = inverse * total[base + 2 : base + 3] * (1.0 / D)
            slope = inverse * inverse * (inverse * product * (1.0 / D))
            exact = jnp.concatenate([inverse, offset, slope, mean], axis=0)
            high = exact.astype(BF).astype(F32)
            middle = (exact - high).astype(BF).astype(F32)
            low = exact - high - middle
            terms.append(jnp.concatenate([high, middle, low, jnp.zeros_like(low)], axis=0).astype(BF))
        return terms

    spread_lane = lax.broadcasted_iota(jnp.int32, (16, 512), 1) >> 7
    spread4 = one_hot(spread_lane == (lax.broadcasted_iota(jnp.int32, (16, 512), 0) & 3))

    def d_attended(i, terms):
        rows = slice(TILE * i, TILE * i + TILE)
        wide = dot_tn(terms, spread4)
        value = (
            wide[:, :128] * da_raw[rows, :].astype(F32)
            - wide[:, 128:256]
            - wide[:, 256:384] * (o_h[rows, :].astype(F32) - wide[:, 384:])
        )
        if i < 4:
            value = jnp.where(tile_row < length - TILE * i, value, 0.0)
        da[rows, :] = value.astype(BF)

    def backward(i):
        rows = slice(TILE * i, TILE * i + TILE)
        count = min(i, 3) + 1
        for j in range(count):
            cols = slice(WIDE * j, WIDE * j + WIDE)
            d_weight = dot_nt(da[rows, :], vst[cols, :])
            dsc[rows, cols] = (d_weight * gst[rows, cols].astype(F32)).astype(BF)
        return (dot(dsc[rows, : WIDE * count], kst[: WIDE * count, :]) * 0.125).astype(BF)

    def grads_send(phase, buf, base):
        place = dqkvu_out.at[:, pl.ds(pl.multiple_of(base + s * 128, 128), 128)]
        seq_send(phase, lambda p: buf.at[rows_at(p, ROWS)], place)
        local(buf.at[rows_at(s, ROWS)], place, LGR)

    got(st_h.at[pl.ds(0, SEQ - 1)], PSH)
    lower, upper = row_terms(st_h)
    for i in range(4):
        d_attended(i, (lower, upper)[i // 2][:, TILE * (i % 2) : TILE * (i % 2) + TILE])
    for i in range(4):
        gq[TILE * i : TILE * i + TILE, :] = backward(i)
    grads_send(PGQ, gq, 2 * D)

    row256 = lax.broadcasted_iota(jnp.int32, (TILE, TILE), 0)
    col256 = lax.broadcasted_iota(jnp.int32, (TILE, TILE), 1)
    perm_core = one_hot(row256 == ((col256 & 127) >> 2) * 8 + (col256 >> 7) * 4 + (col256 & 3))

    def reorder(rows):
        for k in range(NY):
            cols = slice(TILE * k, TILE * k + TILE)
            gated_p[rows, cols] = dot(gated[rows, cols], perm_core).astype(BF)

    def norm(first, gate_ref, gate_first, du_ref):
        rows = pl.ds(pl.multiple_of(first, 32), 32)
        gate_rows = pl.ds(pl.multiple_of(gate_first, 32), 32)
        att = jnp.concatenate([att_r[k, rows, :] for k in range(SEQ)], axis=1).astype(F32)
        centred = att - jnp.mean(att, axis=1, keepdims=True)
        inverse = lax.rsqrt(jnp.mean(centred * centred, axis=1, keepdims=True) + 1e-05)
        normed = centred * inverse
        gate = gate_ref[gate_rows, :].astype(F32)
        gated[rows, :] = (normed * gain[...] * gate).astype(BF)
        scaled = dz[rows, :] * gain[...]
        du_ref[gate_rows, :] = (scaled * normed).astype(BF)

    def norm_hist(r, carry):
        norm(r * 32, u_v, r * 32, du_h)
        return carry

    def norm_tgt(r, carry):
        norm(ROWS + r * 32, tgate, r * 32, dgt)
        return carry

    got(att_r.at[pl.ds(0, 7), pl.ds(0, ROWS)], PAH)
    lax.fori_loop(0, 4, norm_hist, 0)
    local(du_h, dqkvu_out.at[:, pl.ds(0, D)], LDU)
    hist_rows = pl.ds(0, ROWS)
    slot_rows = pl.ds(ROWS, SLOTS)
    reorder(slice(0, ROWS))
    group_send(PGA, hist_rows)

    got(att_r.at[pl.ds(0, 7), pl.ds(ROWS, SLOTS)], PAT)
    lax.fori_loop(0, 2, norm_tgt, 0)
    reorder(slice(ROWS, ROWS + SLOTS))
    group_send(PGB, slot_rows)
    gated_all[mine] = gated_p[:, rows_at(mine, 128)]

    gate_stack = jnp.concatenate([dgt[:, 128 * k : 128 * k + 128] for k in range(SEQ)], axis=0)
    zg[...] = dot(perm_back, gate_stack).astype(BF)
    dp_send(PGT, zg, rg)
    rg[rows_at(g, 16), :] = zg[rows_at(g, 16), :]

    got(cot_all.at[pl.ds(0, NY - 1)], PCO)
    for d in range(1, NY):
        place = cot_all.at[2 * lax.rem(y + d, NY) + core]
        send(place, place, PCF, {"seq": other})

    got(st_t.at[pl.ds(0, SEQ - 1)], PST)
    for i, terms in enumerate(row_terms(st_t)):
        d_attended(4 + i, terms)
    for i in range(4, 6):
        dqt[TILE * (i - 4) : TILE * (i - 3), :] = backward(i)
    seq_send(PQS, lambda p: dqt.at[rows_at(p, SLOTS)], yq.at[rows_at(s, SLOTS)])
    yq[rows_at(s, SLOTS), :] = dqt[rows_at(s, SLOTS), :]

    got(cot_all.at[pl.ds(0, NY)], PCF)
    got(gated_all.at[pl.ds(0, 7), hist_rows], PGA)
    y_own[...] = dot_tn(gated_all[:, :ROWS, :].reshape(8 * ROWS, 128), cot_all[:, :ROWS, :].reshape(8 * ROWS, D))
    got(gated_all.at[pl.ds(0, 7), slot_rows], PGB)
    y_own[...] += dot_tn(gated_all[:, ROWS:, :].reshape(8 * SLOTS, 128), cot_all[:, ROWS:, :].reshape(8 * SLOTS, D))
    for d in range(1, NZ):
        zp = lax.rem(z + d, NZ)
        z_send[zp] = y_own[rows_at(zp, 16), :].astype(BF)
        send(z_send.at[zp], z_recv.at[z], PZ, {"dp": y * NZ + zp})

    def key_sum(left, right, j):
        both = dot_tn(right[TILE * j : ALL, :], left[TILE * j : ALL, WIDE * j : WIDE * j + WIDE])
        return jnp.concatenate([both[:64, :TILE], both[64:, TILE:]], axis=0).T

    for j in range(4):
        gk[TILE * j : TILE * j + TILE, :] = (key_sum(dsc, qs, j) * 2.0).astype(BF)
    grads_send(PGK, gk, 3 * D)
    for j in range(4):
        gv[TILE * j : TILE * j + TILE, :] = key_sum(wst, da, j).astype(BF)
    grads_send(PGV, gv, D)

    got(yq.at[pl.ds(0, 448)], PQS)
    zq[...] = dot(perm_back, yq[...]).astype(BF)
    dp_send(PQD, zq, rq)
    rq[rows_at(g, 16), :] = zq[rows_at(g, 16), :]

    outs[...] = dot(gated[:ROWS, :], w_v[...]).astype(BF)
    local(outs, ho_out, LHO)
    rows32[...] = dot(gated[ROWS:, :], w_v[...])
    for h in range(DP):
        to_v[h] = rows32[2 * h : 2 * h + 2, :].astype(BF)
    local(to_v, to_out, LTO)

    got(z_recv.at[pl.ds(0, NZ - 1)], PZ)
    total = y_own[rows_at(z, 16), :]
    for d in range(1, NZ):
        total = total + z_recv[lax.rem(z + d, NZ)].astype(F32)
    for q in range(4):
        rows = total[4 * q : 4 * q + 4, :]
        x_send[q] = jnp.concatenate([rows[:, :512], rows[:, 512:]], axis=0)
    for d in range(1, 4):
        xp = lax.rem(x + d, 4)
        send(x_send.at[xp], x_recv.at[x], PX, {"seq": 2 * xp + core})
    x_recv[x] = x_send[x]

    got(rg.at[pl.ds(0, 496)], PGT)
    got(rq.at[pl.ds(0, 496)], PQD)
    returned = jnp.concatenate([rq[...], rg[...]], axis=1)
    d_items = dot(sel_t[...], returned).astype(BF)
    for k in range(SEQ):
        di[:, 128 * k : 128 * k + 128] = d_items[64 * k : 64 * k + 64, :128]
        di[:, D + 128 * k : D + 128 * k + 128] = d_items[64 * k : 64 * k + 64, 128:]
    local(di, di_out, LDI)

    got(x_recv.at[pl.ds(0, 3)], PX)
    full = (x_recv[0] + x_recv[1] + x_recv[2] + x_recv[3]) * (32768.0 ** -0.5)
    dw[...] = jnp.concatenate([full[:4, :], full[4:, :]], axis=1)
    local(dw, dw_out, LDW)

    for phase, buf in ((PGQ, gq), (PGK, gk), (PGV, gv)):
        got(buf.at[pl.ds(0, 896)], phase)
        sent(buf.at[pl.ds(0, 896)], phase)
        local_wait(buf.at[pl.ds(0, ROWS)], LGR)
    for phase, buf in ((PK, kraw), (PQ, qraw), (PV, vraw), (PAH, o_h), (PDH, da_raw)):
        sent(buf.at[pl.ds(0, 896)], phase)
    for phase, buf in ((PTQ, tq), (PAT, o_h), (PDT, da_raw), (PQS, dqt)):
        sent(buf.at[pl.ds(0, 448)], phase)
    for phase, buf in ((PT, tsend), (PGT, zg), (PQD, zq)):
        sent(buf.at[pl.ds(0, 496)], phase)
    sent(cot_all.at[pl.ds(0, NY - 1)], PCO)
    sent(cot_all.at[pl.ds(0, NY)], PCF)
    sent(st_h.at[pl.ds(0, SEQ - 1)], PSH)
    sent(st_t.at[pl.ds(0, SEQ - 1)], PST)
    sent(gated_all.at[pl.ds(0, 7), hist_rows], PGA)
    sent(gated_all.at[pl.ds(0, 7), slot_rows], PGB)
    sent(z_send.at[pl.ds(0, NZ - 1)], PZ)
    sent(x_recv.at[pl.ds(0, 3)], PX)
    local_wait(du_h, LDU)
    local_wait(outs, LHO)
    local_wait(to_v, LTO)
    local_wait(di, LDI)
    local_wait(dw, LDW)


def deliver(ho, to, dqkvu, di, dw, ho_out, to_out, dqkvu_out, di_out, dw_out, sem):
    pairs = [(dqkvu.at[pl.ds(32 * r, 32)], dqkvu_out.at[pl.ds(32 * r, 32)]) for r in range(4)]
    pairs += [(ho, ho_out), (to, to_out), (di, di_out), (dw, dw_out)]
    copies = [pltpu.make_async_copy(a, b, sem.at[n]) for n, (a, b) in enumerate(pairs)]
    for copy in copies:
        copy.start()
    for copy in copies:
        copy.wait()


def scratch():
    def vm(*shape, dtype=BF):
        return pltpu.VMEM(shape, dtype)

    return [
        vm(HIST, 128), vm(HIST, 128), vm(ALL, 128), vm(ALL, 128),
        vm(2 * HIST, 128), vm(2 * HIST, 128),
        vm(ALL, 2 * HIST), vm(ALL, 2 * HIST), vm(ALL, 2 * HIST),
        vm(2, DP, dtype=jnp.int32), vm(1, DP, dtype=jnp.int32), vm(SLOTS, 2 * D), vm(1, D, dtype=F32),
        vm(ROWS, D), vm(D, D), vm(DP, 2, D), vm(DP, 2, D), vm(SLOTS, D, dtype=F32),
        vm(ROWS + SLOTS, D), vm(ROWS + SLOTS, D, dtype=F32),
        vm(512, 512), vm(512, 256), vm(512, 256), vm(512, 128), vm(SLOTS, D),
        vm(ALL, 128), vm(SEQ, ROWS + SLOTS, 128), vm(SEQ, ROWS + SLOTS, 128),
        vm(ALL, 128), vm(ALL, 128),
        vm(ROWS + SLOTS, D), vm(ROWS, D), vm(ROWS, D), vm(SLOTS, D),
        vm(512, 128), vm(512, 128), vm(512, 128), vm(512, 128), vm(512, 128), vm(512, 128),
        vm(HIST, 128), vm(HIST, 128), vm(HIST, 128), vm(SLOTS, 2 * D),
        vm(8, 512, dtype=F32), vm(8, TILE, dtype=F32),
        vm(SEQ, 8, 512, dtype=F32), vm(SEQ, 8, TILE, dtype=F32),
        vm(ROWS + SLOTS, D), vm(8, ROWS + SLOTS, D), vm(8, ROWS + SLOTS, 128),
        vm(128, D, dtype=F32), vm(NZ, 16, D), vm(NZ, 16, D),
        vm(4, 8, 512, dtype=F32), vm(4, 8, 512, dtype=F32), vm(4, D, dtype=F32),
        pltpu.SemaphoreType.DMA((NPH,)),
        pltpu.SemaphoreType.DMA((NPH,)),
        pltpu.SemaphoreType.DMA((NLOC,)),
    ]


def shards(qkvu, lengths, items, send_list, send_count, w_out, gain, g_hist, g_tgt):
    hbm = pl.BlockSpec(memory_space=pltpu.HBM)
    vmem = pl.BlockSpec(memory_space=pltpu.VMEM)
    results = pl.pallas_call(
        kernel,
        out_shape=(
            pltpu.VMEM((ROWS, D), BF),
            pltpu.VMEM((DP, 2, D), BF),
            pltpu.VMEM((ROWS, 4 * D), BF),
            pltpu.VMEM((SLOTS, 2 * D), BF),
            pltpu.VMEM((4, D), F32),
        ),
        in_specs=[hbm, hbm, pl.BlockSpec(memory_space=pltpu.SMEM)] + [hbm] * 6,
        out_specs=(vmem,) * 5,
        scratch_shapes=scratch(),
        compiler_params=pltpu.CompilerParams(
            collective_id=0, has_side_effects=True, vmem_limit_bytes=56 * 1024 * 1024
        ),
    )(
        send_list[0, 0].T, send_count[0], lengths, qkvu[0], items[0, 0], w_out, gain.reshape(1, D), g_hist[0], g_tgt[0, 0]
    )
    hist_out, tgt_out, d_qkvu, d_items, d_w2 = pl.pallas_call(
        deliver,
        out_shape=tuple(jax.ShapeDtypeStruct(r.shape, r.dtype) for r in results),
        in_specs=(vmem,) * 5,
        out_specs=(hbm,) * 5,
        scratch_shapes=[pltpu.SemaphoreType.DMA((8,))],
        compiler_params=pltpu.CompilerParams(vmem_limit_bytes=8 * 1024 * 1024),
    )(*results)
    return (
        hist_out[None],
        tgt_out[None, None],
        d_qkvu[None],
        d_items[None, None],
        d_w2,
    )


def solution(mesh):
    in_specs = (
        P("dp", "seq", None),
        P("dp"),
        P("dp", "seq", None, None),
        P("dp", "seq", None, None),
        P("dp", "seq", None),
        P(),
        P(),
        P("dp", "seq", None),
        P("dp", "seq", None, None, None),
    )
    out_specs = (
        P("dp", "seq", None),
        P("dp", "seq", None, None, None),
        P("dp", "seq", None),
        P("dp", "seq", None, None),
        P(("dp", "seq"), None),
    )
    return jax.shard_map(shards, mesh=mesh, in_specs=in_specs, out_specs=out_specs, check_vma=False)
```

```python
import jax
import jax.numpy as jnp
from jax import lax
from jax.experimental import pallas as pl
from jax.experimental.pallas import tpu as pltpu
from jax.sharding import PartitionSpec as P

BF = jnp.bfloat16
F32 = jnp.float32
MESH = pl.DeviceIdType.MESH

D = 1024
SEQ = 8
DP = 32
NY = 4
NZ = 8
ROWS = 128
SLOTS = 64
HIST = 1024
ALL = 1536
TILE = 256
WIDE = 2 * TILE

(PK, PQ, PV, PT, PTQ, PAH, PAT, PDH, PDT, PSH, PST, PGT, PQS, PQD, PGQ, PGK, PGV, PCO, PCF, PGA, PGB, PZ, PX, NPH) = range(24)
(LLI, LCO, LIT, LGA, LIN, LW, LCOT, LGT, LU, LHO, LTO, LDU, LGR, LDI, LDW, NLOC) = range(16)


def dot(a, b):
    return lax.dot_general(a, b, (((1,), (0,)), ((), ())), preferred_element_type=F32)


def dot_nt(a, b):
    return lax.dot_general(a, b, (((1,), (1,)), ((), ())), preferred_element_type=F32)


def dot_tn(a, b):
    return lax.dot_general(a, b, (((0,), (0,)), ((), ())), preferred_element_type=F32)


def one_hot(condition):
    return jnp.where(condition, 1.0, 0.0).astype(BF)


def kernel(
    lists_hbm, counts_hbm, length_ref, qkvu, items_hbm, w_hbm, gain_hbm, gh_hbm, gt_hbm,
    ho_out, to_out, dqkvu_out, di_out, dw_out,
    kraw, vraw, qraw, qs, kst, vst, wst, gst, dsc,
    lists, counts, items, gain, u_v, w_v, gt_v, to_v, rows32, cot, dz, sel_t, tsend, trecv, tq, tgate,
    o_h, att_r, datt, da_raw, da, gated, outs, du_h, dgt, zg, rg, dqt, yq, zq, rq,
    gq, gk, gv, di, st_hs, st_ts, st_h, st_t, gated_p, cot_all, gated_all, y_own, z_send, z_recv, x_send, x_recv, dw,
    ssem, rsem, lsem,
):
    g = lax.axis_index("dp")
    s = lax.axis_index("seq")
    y, z = lax.div(g, NZ), lax.rem(g, NZ)
    x = lax.div(s, 2)
    core = lax.rem(s, 2)
    other = s + 1 - 2 * core
    mine = 2 * y + core
    length = length_ref[0]

    def rows_at(index, size):
        return pl.ds(pl.multiple_of(index * size, size), size)

    barrier = pltpu.get_barrier_semaphore()

    def greet_dp(d, carry):
        pl.semaphore_signal(barrier, inc=1, device_id={"dp": lax.rem(g + d, DP)}, device_id_type=MESH)
        return carry

    for d in range(1, SEQ):
        pl.semaphore_signal(barrier, inc=1, device_id={"seq": lax.rem(s + d, SEQ)}, device_id_type=MESH)
    lax.fori_loop(1, DP, greet_dp, 0)
    for d in range(1, NY):
        pl.semaphore_signal(
            barrier, inc=1, device_id={"dp": lax.rem(y + d, NY) * NZ + z, "seq": other}, device_id_type=MESH
        )

    def local(src, dst, sem):
        copy = pltpu.make_async_copy(src, dst, lsem.at[sem])
        copy.start()

    def local_wait(ref, sem):
        pltpu.make_async_copy(ref, ref, lsem.at[sem]).wait()

    def send(src, dst, phase, device):
        pltpu.make_async_remote_copy(
            src_ref=src, dst_ref=dst, send_sem=ssem.at[phase], recv_sem=rsem.at[phase],
            device_id=device, device_id_type=MESH,
        ).start()

    def seq_send(phase, src, dst):
        for d in range(1, SEQ):
            p = lax.rem(s + d, SEQ)
            send(src(p), dst, phase, {"seq": p})

    def got(ref, phase):
        pltpu.make_async_copy(ref, ref, rsem.at[phase]).wait()

    def sent(ref, phase):
        pltpu.make_async_copy(ref, ref, ssem.at[phase]).wait()

    local(lists_hbm, lists, LLI)
    local(counts_hbm, counts, LCO)
    local(items_hbm, items, LIT)
    local(gain_hbm, gain, LGA)
    for base, buf in ((3 * D, kraw), (2 * D, qraw), (D, vraw)):
        local(qkvu.at[:, pl.ds(pl.multiple_of(base + s * 128, 128), 128)], buf.at[rows_at(s, ROWS)], LIN)
    local(w_hbm, w_v, LW)
    local(gh_hbm, cot.at[pl.ds(0, ROWS)], LCOT)
    local(gt_hbm, gt_v, LGT)
    local(qkvu.at[:, pl.ds(0, D)], u_v, LU)

    local_wait(lists, LLI)
    local_wait(counts, LCO)
    lane512 = lax.broadcasted_iota(jnp.int32, (DP, 512), 1)
    spread = one_hot((lane512 >> 4) == lax.broadcasted_iota(jnp.int32, (DP, 512), 0))

    def spread_row(row):
        return dot(jnp.broadcast_to(row.astype(F32), (16, DP)).astype(BF), spread)[:1, :]

    slot = lax.broadcasted_iota(jnp.int32, (1, 512), 1)
    second = (slot & 1) == 1
    picked = jnp.where(second, spread_row(lists[1:2, :]), spread_row(lists[0:1, :]))
    live = spread_row(counts[...]) > jnp.where(second, 1.5, 0.5)
    code = jnp.where(live, picked + (((slot >> 1) & 7) * SLOTS).astype(F32), -1.0)
    sel_t[...] = one_hot(lax.broadcasted_iota(jnp.int32, (512, 512), 0).astype(F32) == code)
    local_wait(items, LIT)
    stacked = jnp.concatenate(
        [
            jnp.concatenate([items[:, 128 * k : 128 * k + 128], items[:, D + 128 * k : D + 128 * k + 128]], axis=1)
            for k in range(SEQ)
        ],
        axis=0,
    )
    tsend[...] = dot_tn(sel_t[...], stacked).astype(BF)

    pl.semaphore_wait(barrier, SEQ - 1 + DP - 1 + NY - 1)

    def dp_send(phase, src, dst):
        def one(d, carry):
            p = lax.rem(g + d, DP)
            send(src.at[rows_at(p, 16)], dst.at[rows_at(g, 16)], phase, {"dp": p})
            return carry

        lax.fori_loop(1, DP, one, 0)

    def columns_send(phase, base, buf):
        seq_send(
            phase, lambda p: qkvu.at[:, pl.ds(pl.multiple_of(base + p * 128, 128), 128)], buf.at[rows_at(s, ROWS)]
        )

    columns_send(PK, 3 * D, kraw)
    dp_send(PT, tsend, trecv)
    columns_send(PQ, 2 * D, qraw)
    columns_send(PV, D, vraw)
    trecv[rows_at(g, 16), :] = tsend[rows_at(g, 16), :]

    local_wait(w_v, LW)
    local_wait(cot.at[pl.ds(0, ROWS)], LCOT)
    local_wait(gt_v, LGT)
    for h in range(DP):
        rows32[2 * h : 2 * h + 2, :] = gt_v[h].astype(F32)
    cot[ROWS:, :] = rows32[...].astype(BF)
    for d in range(1, NY):
        send(cot, cot_all.at[mine], PCO, {"dp": lax.rem(y + d, NY) * NZ + z})
    send(cot, cot_all.at[mine], PCF, {"seq": other})
    dz[...] = dot_nt(cot[...], w_v[...])

    def d_norm(first, gate_ref, gate_first):
        rows = pl.ds(pl.multiple_of(first, 32), 32)
        gate = gate_ref[pl.ds(pl.multiple_of(gate_first, 32), 32), :].astype(F32)
        value = (dz[rows, :] * gain[...] * gate).astype(BF)
        for k in range(SEQ):
            datt[k, rows, :] = value[:, 128 * k : 128 * k + 128]

    def d_norm_hist(r, carry):
        d_norm(r * 32, u_v, r * 32)
        return carry

    def d_norm_tgt(r, carry):
        d_norm(ROWS + r * 32, tgate, r * 32)
        return carry

    target_rows = pl.ds(pl.multiple_of(HIST + s * SLOTS, SLOTS), SLOTS)
    local_wait(u_v, LU)
    local_wait(gain, LGA)
    lax.fori_loop(0, 4, d_norm_hist, 0)
    seq_send(PDH, lambda p: datt.at[p, pl.ds(0, ROWS)], da_raw.at[rows_at(s, ROWS)])
    da_raw[rows_at(s, ROWS), :] = datt[s, pl.ds(0, ROWS), :]

    row512 = lax.broadcasted_iota(jnp.int32, (512, 512), 0)
    col512 = lax.broadcasted_iota(jnp.int32, (512, 512), 1)
    perm = one_hot(col512 == ((row512 & 63) >> 1) * 16 + (row512 >> 6) * 2 + (row512 & 1))
    perm_back = one_hot(row512 == ((col512 & 63) >> 1) * 16 + (col512 >> 6) * 2 + (col512 & 1))

    got(trecv.at[pl.ds(0, 496)], PT)
    arranged = dot(perm, trecv[...]).astype(BF)
    tq[...] = arranged[:, :128]
    for k in range(SEQ):
        tgate[:, 128 * k : 128 * k + 128] = arranged[64 * k : 64 * k + 64, 128:]
    seq_send(PTQ, lambda p: tq.at[rows_at(p, SLOTS)], qraw.at[target_rows])
    qraw[target_rows, :] = tq[rows_at(s, SLOTS), :]

    lax.fori_loop(0, 2, d_norm_tgt, 0)
    seq_send(PDT, lambda p: datt.at[p, pl.ds(ROWS, SLOTS)], da_raw.at[target_rows])
    da_raw[target_rows, :] = datt[s, pl.ds(ROWS, SLOTS), :]
    cot_all[mine] = cot[...]

    def group_send(phase, rows):
        for d in range(1, 2 * NY):
            r = lax.rem(mine + d, 2 * NY)
            send(
                gated_p.at[rows, rows_at(r, 128)], gated_all.at[mine, rows], phase,
                {"dp": lax.div(r, 2) * NZ + z, "seq": s - core + lax.rem(r, 2)},
            )

    for buf in (kraw, qraw, vraw):
        local_wait(buf.at[pl.ds(0, ROWS)], LIN)
    lane = lax.broadcasted_iota(jnp.int32, (TILE, 128), 1)
    tile_row = lax.broadcasted_iota(jnp.int32, (TILE, 128), 0)

    def stack_heads(raw, out):
        for j in range(4):
            block = raw[TILE * j : TILE * j + TILE, :].astype(F32)
            live = tile_row < length - TILE * j
            out[WIDE * j : WIDE * j + TILE, :] = jnp.where(live & (lane < 64), block, 0.0).astype(BF)
            out[WIDE * j + TILE : WIDE * j + WIDE, :] = jnp.where(live & (lane >= 64), block, 0.0).astype(BF)

    got(kraw.at[pl.ds(0, 896)], PK)
    stack_heads(kraw, kst)
    got(qraw.at[pl.ds(0, 896)], PQ)
    for i in range(4):
        block = qraw[TILE * i : TILE * i + TILE, :].astype(F32) * 0.0625
        qs[TILE * i : TILE * i + TILE, :] = jnp.where(tile_row < length - TILE * i, block, 0.0).astype(BF)

    causal = (lax.broadcasted_iota(jnp.int32, (TILE, WIDE), 1) & (TILE - 1)) <= lax.broadcasted_iota(
        jnp.int32, (TILE, WIDE), 0
    )

    def scores(i):
        rows = slice(TILE * i, TILE * i + TILE)
        count = min(i, 3) + 1
        for j in range(count):
            cols = slice(WIDE * j, WIDE * j + WIDE)
            half = dot_nt(qs[rows, :], kst[cols, :])
            twice = 1.0 + jnp.tanh(half)
            weight = half * twice
            slope = 0.5 * twice * (1.0 - weight) + weight
            if i == j:
                weight = jnp.where(causal, weight, 0.0)
                slope = jnp.where(causal, slope, 0.0)
            wst[rows, cols] = weight.astype(BF)
            gst[rows, cols] = slope.astype(BF)

    def attend(i):
        rows = slice(TILE * i, TILE * i + TILE)
        count = min(i, 3) + 1
        o_h[rows, :] = dot(wst[rows, : WIDE * count], vst[: WIDE * count, :]).astype(BF)

    for i in range(4):
        scores(i)
    got(vraw.at[pl.ds(0, 896)], PV)
    stack_heads(vraw, vst)
    for i in range(4):
        attend(i)

    ones = jnp.ones((128, 128), BF)
    stat_row = lax.broadcasted_iota(jnp.int32, (16, 128), 0)

    def two(value):
        high = value.astype(BF)
        return high, (value - high.astype(F32)).astype(BF)

    def stats(i, base):
        rows = slice(TILE * i, TILE * i + TILE)
        att, dn = o_h[rows, :], da_raw[rows, :]
        centred = att.astype(F32) - dot(att, ones) * (1.0 / 128.0)
        parts = [(0, att), (2, dn)]
        parts += [(1, part) for part in two(centred * centred)]
        parts += [(3, part) for part in two(centred * dn.astype(F32))]
        total = dot_nt(one_hot(stat_row == base + parts[0][0]), parts[0][1])
        for q, part in parts[1:]:
            total = total + dot_nt(one_hot(stat_row == base + q), part)
        return total[:8, :]

    got(da_raw.at[pl.ds(0, 896)], PDH)
    st_hs[:, :TILE] = stats(0, 0) + stats(2, 4)
    st_hs[:, TILE:] = stats(1, 0) + stats(3, 4)
    seq_send(PSH, lambda p: st_hs, st_h.at[s])
    st_h[s] = st_hs[...]
    seq_send(PAH, lambda p: o_h.at[rows_at(p, ROWS)], att_r.at[s, pl.ds(0, ROWS)])
    att_r[s, pl.ds(0, ROWS), :] = o_h[rows_at(s, ROWS), :]

    got(qraw.at[pl.ds(HIST, 448)], PTQ)
    for i in range(4, 6):
        rows = slice(TILE * i, TILE * i + TILE)
        qs[rows, :] = (qraw[rows, :].astype(F32) * 0.0625).astype(BF)
        scores(i)
        attend(i)
    seq_send(
        PAT,
        lambda p: o_h.at[pl.ds(pl.multiple_of(HIST + p * SLOTS, SLOTS), SLOTS)],
        att_r.at[s, pl.ds(ROWS, SLOTS)],
    )
    got(da_raw.at[pl.ds(HIST, 448)], PDT)
    st_ts[...] = stats(4, 0) + stats(5, 4)
    seq_send(PST, lambda p: st_ts, st_t.at[s])
    st_t[s] = st_ts[...]
    att_r[s, pl.ds(ROWS, SLOTS), :] = o_h[target_rows, :]

    def row_terms(received):
        blocks = [received[k] for k in range(SEQ)]
        total = blocks[0]
        for block in blocks[1:]:
            total = total + block
        terms = []
        for base in (0, 4):
            mean = total[base : base + 1] * (1.0 / D)
            squares, product = total[base + 1 : base + 2], total[base + 3 : base + 4]
            for block in blocks:
                shift = block[base : base + 1] * (1.0 / 128.0) - mean
                squares = squares + 128.0 * shift * shift
                product = product + block[base + 2 : base + 3] * shift
            inverse = lax.rsqrt(squares * (1.0 / D) + 1e-05)
            offset = inverse * total[base + 2 : base + 3] * (1.0 / D)
            slope = inverse * inverse * (inverse * product * (1.0 / D))
            exact = jnp.concatenate([inverse, offset, slope, mean], axis=0)
            high = exact.astype(BF).astype(F32)
            middle = (exact - high).astype(BF).astype(F32)
            low = exact - high - middle
            terms.append(jnp.concatenate([high, middle, low, jnp.zeros_like(low)], axis=0).astype(BF))
        return terms

    spread_lane = lax.broadcasted_iota(jnp.int32, (16, 512), 1) >> 7
    spread4 = one_hot(spread_lane == (lax.broadcasted_iota(jnp.int32, (16, 512), 0) & 3))

    def d_attended(i, terms):
        rows = slice(TILE * i, TILE * i + TILE)
        wide = dot_tn(terms, spread4)
        value = (
            wide[:, :128] * da_raw[rows, :].astype(F32)
            - wide[:, 128:256]
            - wide[:, 256:384] * (o_h[rows, :].astype(F32) - wide[:, 384:])
        )
        if i < 4:
            value = jnp.where(tile_row < length - TILE * i, value, 0.0)
        da[rows, :] = value.astype(BF)

    def backward(i):
        rows = slice(TILE * i, TILE * i + TILE)
        count = min(i, 3) + 1
        for j in range(count):
            cols = slice(WIDE * j, WIDE * j + WIDE)
            d_weight = dot_nt(da[rows, :], vst[cols, :])
            dsc[rows, cols] = (d_weight * gst[rows, cols].astype(F32)).astype(BF)
        return (dot(dsc[rows, : WIDE * count], kst[: WIDE * count, :]) * 0.125).astype(BF)

    def grads_send(phase, buf, base):
        place = dqkvu_out.at[:, pl.ds(pl.multiple_of(base + s * 128, 128), 128)]
        seq_send(phase, lambda p: buf.at[rows_at(p, ROWS)], place)
        local(buf.at[rows_at(s, ROWS)], place, LGR)

    got(st_h.at[pl.ds(0, SEQ - 1)], PSH)
    lower, upper = row_terms(st_h)
    for i in range(4):
        d_attended(i, (lower, upper)[i // 2][:, TILE * (i % 2) : TILE * (i % 2) + TILE])
    for i in range(4):
        gq[TILE * i : TILE * i + TILE, :] = backward(i)
    grads_send(PGQ, gq, 2 * D)
    got(cot_all.at[pl.ds(0, NY - 1)], PCO)
    for d in range(1, NY):
        place = cot_all.at[2 * lax.rem(y + d, NY) + core]
        send(place, place, PCF, {"seq": other})


    row256 = lax.broadcasted_iota(jnp.int32, (TILE, TILE), 0)
    col256 = lax.broadcasted_iota(jnp.int32, (TILE, TILE), 1)
    perm_core = one_hot(row256 == ((col256 & 127) >> 2) * 8 + (col256 >> 7) * 4 + (col256 & 3))

    def reorder(rows):
        for k in range(NY):
            cols = slice(TILE * k, TILE * k + TILE)
            gated_p[rows, cols] = dot(gated[rows, cols], perm_core).astype(BF)

    def norm(first, gate_ref, gate_first, du_ref):
        rows = pl.ds(pl.multiple_of(first, 32), 32)
        gate_rows = pl.ds(pl.multiple_of(gate_first, 32), 32)
        att = jnp.concatenate([att_r[k, rows, :] for k in range(SEQ)], axis=1).astype(F32)
        centred = att - jnp.mean(att, axis=1, keepdims=True)
        inverse = lax.rsqrt(jnp.mean(centred * centred, axis=1, keepdims=True) + 1e-05)
        normed = centred * inverse
        gate = gate_ref[gate_rows, :].astype(F32)
        gated[rows, :] = (normed * gain[...] * gate).astype(BF)
        scaled = dz[rows, :] * gain[...]
        du_ref[gate_rows, :] = (scaled * normed).astype(BF)

    def norm_hist(r, carry):
        norm(r * 32, u_v, r * 32, du_h)
        return carry

    def norm_tgt(r, carry):
        norm(ROWS + r * 32, tgate, r * 32, dgt)
        return carry

    got(att_r.at[pl.ds(0, 7), pl.ds(0, ROWS)], PAH)
    lax.fori_loop(0, 4, norm_hist, 0)
    local(du_h, dqkvu_out.at[:, pl.ds(0, D)], LDU)
    hist_rows = pl.ds(0, ROWS)
    slot_rows = pl.ds(ROWS, SLOTS)
    reorder(slice(0, ROWS))
    group_send(PGA, hist_rows)

    got(att_r.at[pl.ds(0, 7), pl.ds(ROWS, SLOTS)], PAT)
    lax.fori_loop(0, 2, norm_tgt, 0)
    reorder(slice(ROWS, ROWS + SLOTS))
    group_send(PGB, slot_rows)
    gated_all[mine] = gated_p[:, rows_at(mine, 128)]

    gate_stack = jnp.concatenate([dgt[:, 128 * k : 128 * k + 128] for k in range(SEQ)], axis=0)
    zg[...] = dot(perm_back, gate_stack).astype(BF)
    dp_send(PGT, zg, rg)
    rg[rows_at(g, 16), :] = zg[rows_at(g, 16), :]

    got(st_t.at[pl.ds(0, SEQ - 1)], PST)
    for i, terms in enumerate(row_terms(st_t)):
        d_attended(4 + i, terms)
    for i in range(4, 6):
        dqt[TILE * (i - 4) : TILE * (i - 3), :] = backward(i)
    seq_send(PQS, lambda p: dqt.at[rows_at(p, SLOTS)], yq.at[rows_at(s, SLOTS)])
    yq[rows_at(s, SLOTS), :] = dqt[rows_at(s, SLOTS), :]

    got(cot_all.at[pl.ds(0, NY)], PCF)
    got(gated_all.at[pl.ds(0, 7), hist_rows], PGA)
    y_own[...] = dot_tn(gated_all[:, :ROWS, :].reshape(8 * ROWS, 128), cot_all[:, :ROWS, :].reshape(8 * ROWS, D))
    got(gated_all.at[pl.ds(0, 7), slot_rows], PGB)
    y_own[...] += dot_tn(gated_all[:, ROWS:, :].reshape(8 * SLOTS, 128), cot_all[:, ROWS:, :].reshape(8 * SLOTS, D))
    for d in range(1, NZ):
        zp = lax.rem(z + d, NZ)
        z_send[zp] = y_own[rows_at(zp, 16), :].astype(BF)
        send(z_send.at[zp], z_recv.at[z], PZ, {"dp": y * NZ + zp})

    def key_sum(left, right, j):
        both = dot_tn(right[TILE * j : ALL, :], left[TILE * j : ALL, WIDE * j : WIDE * j + WIDE])
        return jnp.concatenate([both[:64, :TILE], both[64:, TILE:]], axis=0).T

    for j in range(4):
        gk[TILE * j : TILE * j + TILE, :] = (key_sum(dsc, qs, j) * 2.0).astype(BF)
    grads_send(PGK, gk, 3 * D)
    for j in range(4):
        gv[TILE * j : TILE * j + TILE, :] = key_sum(wst, da, j).astype(BF)
    grads_send(PGV, gv, D)

    got(yq.at[pl.ds(0, 448)], PQS)
    zq[...] = dot(perm_back, yq[...]).astype(BF)
    dp_send(PQD, zq, rq)
    rq[rows_at(g, 16), :] = zq[rows_at(g, 16), :]

    outs[...] = dot(gated[:ROWS, :], w_v[...]).astype(BF)
    local(outs, ho_out, LHO)
    rows32[...] = dot(gated[ROWS:, :], w_v[...])
    for h in range(DP):
        to_v[h] = rows32[2 * h : 2 * h + 2, :].astype(BF)
    local(to_v, to_out, LTO)

    got(z_recv.at[pl.ds(0, NZ - 1)], PZ)
    total = y_own[rows_at(z, 16), :]
    for d in range(1, NZ):
        total = total + z_recv[lax.rem(z + d, NZ)].astype(F32)
    for q in range(4):
        rows = total[4 * q : 4 * q + 4, :]
        x_send[q] = jnp.concatenate([rows[:, :512], rows[:, 512:]], axis=0)
    for d in range(1, 4):
        xp = lax.rem(x + d, 4)
        send(x_send.at[xp], x_recv.at[x], PX, {"seq": 2 * xp + core})
    x_recv[x] = x_send[x]

    got(rg.at[pl.ds(0, 496)], PGT)
    got(rq.at[pl.ds(0, 496)], PQD)
    returned = jnp.concatenate([rq[...], rg[...]], axis=1)
    d_items = dot(sel_t[...], returned).astype(BF)
    for k in range(SEQ):
        di[:, 128 * k : 128 * k + 128] = d_items[64 * k : 64 * k + 64, :128]
        di[:, D + 128 * k : D + 128 * k + 128] = d_items[64 * k : 64 * k + 64, 128:]
    local(di, di_out, LDI)

    got(x_recv.at[pl.ds(0, 3)], PX)
    full = (x_recv[0] + x_recv[1] + x_recv[2] + x_recv[3]) * (32768.0 ** -0.5)
    dw[...] = jnp.concatenate([full[:4, :], full[4:, :]], axis=1)
    local(dw, dw_out, LDW)

    for phase, buf in ((PGQ, gq), (PGK, gk), (PGV, gv)):
        got(buf.at[pl.ds(0, 896)], phase)
        sent(buf.at[pl.ds(0, 896)], phase)
        local_wait(buf.at[pl.ds(0, ROWS)], LGR)
    for phase, buf in ((PK, kraw), (PQ, qraw), (PV, vraw), (PAH, o_h), (PDH, da_raw)):
        sent(buf.at[pl.ds(0, 896)], phase)
    for phase, buf in ((PTQ, tq), (PAT, o_h), (PDT, da_raw), (PQS, dqt)):
        sent(buf.at[pl.ds(0, 448)], phase)
    for phase, buf in ((PT, tsend), (PGT, zg), (PQD, zq)):
        sent(buf.at[pl.ds(0, 496)], phase)
    sent(cot_all.at[pl.ds(0, NY - 1)], PCO)
    sent(cot_all.at[pl.ds(0, NY)], PCF)
    sent(st_h.at[pl.ds(0, SEQ - 1)], PSH)
    sent(st_t.at[pl.ds(0, SEQ - 1)], PST)
    sent(gated_all.at[pl.ds(0, 7), hist_rows], PGA)
    sent(gated_all.at[pl.ds(0, 7), slot_rows], PGB)
    sent(z_send.at[pl.ds(0, NZ - 1)], PZ)
    sent(x_recv.at[pl.ds(0, 3)], PX)
    local_wait(du_h, LDU)
    local_wait(outs, LHO)
    local_wait(to_v, LTO)
    local_wait(di, LDI)
    local_wait(dw, LDW)


def deliver(ho, to, dqkvu, di, dw, ho_out, to_out, dqkvu_out, di_out, dw_out, sem):
    pairs = [(dqkvu.at[pl.ds(32 * r, 32)], dqkvu_out.at[pl.ds(32 * r, 32)]) for r in range(4)]
    pairs += [(ho, ho_out), (to, to_out), (di, di_out), (dw, dw_out)]
    copies = [pltpu.make_async_copy(a, b, sem.at[n]) for n, (a, b) in enumerate(pairs)]
    for copy in copies:
        copy.start()
    for copy in copies:
        copy.wait()


def scratch():
    def vm(*shape, dtype=BF):
        return pltpu.VMEM(shape, dtype)

    return [
        vm(HIST, 128), vm(HIST, 128), vm(ALL, 128), vm(ALL, 128),
        vm(2 * HIST, 128), vm(2 * HIST, 128),
        vm(ALL, 2 * HIST), vm(ALL, 2 * HIST), vm(ALL, 2 * HIST),
        vm(2, DP, dtype=jnp.int32), vm(1, DP, dtype=jnp.int32), vm(SLOTS, 2 * D), vm(1, D, dtype=F32),
        vm(ROWS, D), vm(D, D), vm(DP, 2, D), vm(DP, 2, D), vm(SLOTS, D, dtype=F32),
        vm(ROWS + SLOTS, D), vm(ROWS + SLOTS, D, dtype=F32),
        vm(512, 512), vm(512, 256), vm(512, 256), vm(512, 128), vm(SLOTS, D),
        vm(ALL, 128), vm(SEQ, ROWS + SLOTS, 128), vm(SEQ, ROWS + SLOTS, 128),
        vm(ALL, 128), vm(ALL, 128),
        vm(ROWS + SLOTS, D), vm(ROWS, D), vm(ROWS, D), vm(SLOTS, D),
        vm(512, 128), vm(512, 128), vm(512, 128), vm(512, 128), vm(512, 128), vm(512, 128),
        vm(HIST, 128), vm(HIST, 128), vm(HIST, 128), vm(SLOTS, 2 * D),
        vm(8, 512, dtype=F32), vm(8, TILE, dtype=F32),
        vm(SEQ, 8, 512, dtype=F32), vm(SEQ, 8, TILE, dtype=F32),
        vm(ROWS + SLOTS, D), vm(8, ROWS + SLOTS, D), vm(8, ROWS + SLOTS, 128),
        vm(128, D, dtype=F32), vm(NZ, 16, D), vm(NZ, 16, D),
        vm(4, 8, 512, dtype=F32), vm(4, 8, 512, dtype=F32), vm(4, D, dtype=F32),
        pltpu.SemaphoreType.DMA((NPH,)),
        pltpu.SemaphoreType.DMA((NPH,)),
        pltpu.SemaphoreType.DMA((NLOC,)),
    ]


def shards(qkvu, lengths, items, send_list, send_count, w_out, gain, g_hist, g_tgt):
    hbm = pl.BlockSpec(memory_space=pltpu.HBM)
    vmem = pl.BlockSpec(memory_space=pltpu.VMEM)
    results = pl.pallas_call(
        kernel,
        out_shape=(
            pltpu.VMEM((ROWS, D), BF),
            pltpu.VMEM((DP, 2, D), BF),
            pltpu.VMEM((ROWS, 4 * D), BF),
            pltpu.VMEM((SLOTS, 2 * D), BF),
            pltpu.VMEM((4, D), F32),
        ),
        in_specs=[hbm, hbm, pl.BlockSpec(memory_space=pltpu.SMEM)] + [hbm] * 6,
        out_specs=(vmem,) * 5,
        scratch_shapes=scratch(),
        compiler_params=pltpu.CompilerParams(
            collective_id=0, has_side_effects=True, vmem_limit_bytes=56 * 1024 * 1024
        ),
    )(
        send_list[0, 0].T, send_count[0], lengths, qkvu[0], items[0, 0], w_out, gain.reshape(1, D), g_hist[0], g_tgt[0, 0]
    )
    hist_out, tgt_out, d_qkvu, d_items, d_w2 = pl.pallas_call(
        deliver,
        out_shape=tuple(jax.ShapeDtypeStruct(r.shape, r.dtype) for r in results),
        in_specs=(vmem,) * 5,
        out_specs=(hbm,) * 5,
        scratch_shapes=[pltpu.SemaphoreType.DMA((8,))],
        compiler_params=pltpu.CompilerParams(vmem_limit_bytes=8 * 1024 * 1024),
    )(*results)
    return (
        hist_out[None],
        tgt_out[None, None],
        d_qkvu[None],
        d_items[None, None],
        d_w2,
    )


def solution(mesh):
    in_specs = (
        P("dp", "seq", None),
        P("dp"),
        P("dp", "seq", None, None),
        P("dp", "seq", None, None),
        P("dp", "seq", None),
        P(),
        P(),
        P("dp", "seq", None),
        P("dp", "seq", None, None, None),
    )
    out_specs = (
        P("dp", "seq", None),
        P("dp", "seq", None, None, None),
        P("dp", "seq", None),
        P("dp", "seq", None, None),
        P(("dp", "seq"), None),
    )
    return jax.shard_map(shards, mesh=mesh, in_specs=in_specs, out_specs=out_specs, check_vma=False)
```
